768 devices in a mesh: row: 8 (over y), inner: 6 (over z_lo), out: 16 (over z_hi, x, core).
Axes of the slice: x: 4, y: 8, z: 12 (z_hi: 2, z_lo: 6; z = z_hi * 6 + z_lo), core: 2. Of those that a mesh axis runs over, the one named last changes fastest.
Arguments:
- tokens: bfloat16 [384, 8192], P(('inner', 'out'), 'row'), may hold values from -6 to 6
- grad_out: bfloat16 [384, 8192], P(('inner', 'out'), 'row'), may hold values from -6 to 6
- gate_weight: bfloat16 [8192, 24576], P('row', ('inner', 'out')), may hold values from -0.0625 to 0.0625
- up_weight: bfloat16 [8192, 24576], P('row', ('inner', 'out')), may hold values from -0.0625 to 0.0625
- down_weight: bfloat16 [24576, 8192], P(('inner', 'out'), 'row'), may hold values from -0.0390625 to 0.0390625
Outputs:
- mixed: bfloat16 [384, 8192], P(('inner', 'out'), 'row')
- grad_tokens: bfloat16 [384, 8192], P(('inner', 'out'), 'row')
- grad_gate: bfloat16 [8192, 24576], P('row', ('inner', 'out'))
- grad_up: bfloat16 [8192, 24576], P('row', ('inner', 'out'))
- grad_down: bfloat16 [24576, 8192], P(('inner', 'out'), 'row')
The draws below stay inside these ranges and needn't reach their ends.
All inputs are finite; a program needn't handle non-finite values.
Results may differ from the reference program's by a relative error of at most 0.005.
Values may be sent and summed in bfloat16 or wider, within the bound.
A program may use at most 32 MiB of HBM per device.

```python
import jax
import jax.numpy as jnp

D = 8192
FF = 24576
TOKENS = 384


def level_of(key, dims, shards, least, largest):
    def one(dim, parts):
        steps = jax.random.uniform(jax.random.fold_in(jax.random.fold_in(key, 6), dim), (parts,), jnp.float32, least / len(shards), largest / len(shards))
        return jnp.repeat(jnp.exp(steps), dims[dim] // parts).reshape((-1,) + (1,) * (len(dims) - dim - 1))

    level = one(*shards[0])
    for cut in shards[1:]:
        level = level * one(*cut)
    return level


def normal_values(key, dims, scale, reach, shards=(), held_as=jnp.bfloat16):
    result = scale * jax.random.normal(key, dims, jnp.float32)
    if shards:
        result = result * level_of(key, dims, shards, -0.22, 0.18)
    return jnp.clip(result, -reach, reach).astype(held_as)


def setup_inputs(seed: int = 0) -> dict:
    splits = jax.random.split(jax.random.key(seed), 6)
    tokens = normal_values(splits[0], (TOKENS, D), 1.0, 6.0, ((0, 96), (1, 8)))
    grad_out = normal_values(splits[1], (TOKENS, D), 1.0, 6.0, ((0, 96), (1, 8)))
    gate_weight = normal_values(splits[2], (D, FF), D ** -0.5, 0.0625, ((0, 8), (1, 96)))
    up_weight = normal_values(splits[3], (D, FF), D ** -0.5, 0.0625, ((0, 8), (1, 96)))
    down_weight = normal_values(splits[4], (FF, D), FF ** -0.5, 0.0390625, ((0, 96), (1, 8)))
    return dict(tokens=tokens, grad_out=grad_out, gate_weight=gate_weight, up_weight=up_weight, down_weight=down_weight)


def reference(tokens, grad_out, gate_weight, up_weight, down_weight):
    gate = jnp.dot(tokens, gate_weight, preferred_element_type=jnp.float32)
    up = jnp.dot(tokens, up_weight, preferred_element_type=jnp.float32)
    back = jnp.dot(grad_out, down_weight.T, preferred_element_type=jnp.float32)
    sig = jax.nn.sigmoid(gate)
    hidden = (gate * sig * up).astype(jnp.bfloat16)
    d_up = (back * gate * sig).astype(jnp.bfloat16)
    d_gate = (back * up * sig * (1.0 + gate * (1.0 - sig))).astype(jnp.bfloat16)
    mixed = jnp.dot(hidden, down_weight, preferred_element_type=jnp.float32).astype(jnp.bfloat16)
    grad_tokens = (jnp.dot(d_gate, gate_weight.T, preferred_element_type=jnp.float32)
                   + jnp.dot(d_up, up_weight.T, preferred_element_type=jnp.float32)).astype(jnp.bfloat16)
    grad_gate = jnp.dot(tokens.T, d_gate, preferred_element_type=jnp.float32).astype(jnp.bfloat16)
    grad_up = jnp.dot(tokens.T, d_up, preferred_element_type=jnp.float32).astype(jnp.bfloat16)
    grad_down = jnp.dot(hidden.T, grad_out, preferred_element_type=jnp.float32).astype(jnp.bfloat16)
    return mixed, grad_tokens, grad_gate, grad_up, grad_down
```

```python
import functools

import jax
import jax.numpy as jnp
from jax import lax
from jax.experimental import pallas as pl
from jax.experimental.pallas import tpu as pltpu
from jax.sharding import PartitionSpec as P

MESH = pl.DeviceIdType.MESH
BF16, F32 = jnp.bfloat16, jnp.float32

NX, NY, NZ = 4, 8, 12
Z_LO = 6
TB = 4
D = 1024
F = 256
CT = NZ * TB
ROWS, LANES = CT // 2, 128
ORDER = (0, 1, 3, 2)


def dot(a, b):
    return jnp.dot(a, b, preferred_element_type=F32)


def dot_nt(a, b):
    return lax.dot_general(a, b, (((1,), (1,)), ((), ())), preferred_element_type=F32)


def dot_tn(a, b):
    return lax.dot_general(a, b, (((0,), (0,)), ((), ())), preferred_element_type=F32)


def kernel(
    tok, gout, wg_in, wu_in, wd_in,
    mixed, gtok, ggate, gup, gdown,
    X, Wg, Wu, Wd, T, G, S1, R1, R2, H, HP, SX, RX, OX, SZ, RZ, A1, A2, A3,
    w_sem, wx_send, wx_recv, z_send, z_recv, x_send, x_recv, t_send, t_recv,
    y1_send, y1_recv, y2_send, y2_recv, h_send, h_recv,
    rx_send, rx_recv, rz_send, rz_recv, o_sem,
):
    y = lax.axis_index("row")
    z = lax.axis_index("inner")
    o = lax.axis_index("out")
    core = lax.rem(o, 2)
    x = lax.rem(o // 2, NX)
    z = z + Z_LO * (o // (2 * NX))

    def at(dx=0, dy=0, dz=0, dc=0):
        xx = lax.rem(x + dx, NX)
        zz = lax.rem(z + dz, NZ)
        cc = lax.rem(core + dc, 2)
        return (
            lax.rem(y + dy, NY),
            lax.rem(zz, Z_LO),
            ((zz // Z_LO) * NX + xx) * 2 + cc,
        )

    def send(src, dst, ssem, rsem, to):
        copy = pltpu.make_async_remote_copy(
            src_ref=src, dst_ref=dst, send_sem=ssem, recv_sem=rsem,
            device_id=to, device_id_type=MESH,
        )
        copy.start()

    def wait(ref, sem):
        pltpu.make_async_copy(ref, ref, sem).wait()

    barrier = pltpu.get_barrier_semaphore()
    peers = (
        [at(dz=d) for d in range(1, NZ)]
        + [at(dx=d) for d in range(1, NX)]
        + [at(dy=d) for d in range(1, NY)]
        + [at(dc=1)]
    )
    for peer in peers:
        pl.semaphore_signal(barrier, inc=1, device_id=peer, device_id_type=MESH)

    weights = ((wg_in, Wg), (wu_in, Wu), (wd_in, Wd))
    for i, (src, dst) in enumerate(weights):
        pltpu.make_async_copy(src, dst.at[0], w_sem.at[i]).start()

    X[0, 0] = jnp.concatenate([tok[...].astype(F32), gout[...].astype(F32)], axis=0).astype(BF16)

    pl.semaphore_wait(barrier, len(peers))

    near = [1, 11, 2, 10, 3, 9, 4, 8, 5, 7, 6]

    def to_x(dz):
        for dx in (1, 3, 2):
            send(X.at[0, dz], X.at[NX - dx, dz], x_send, x_recv.at[NX - dx - 1], at(dx=dx))

    for dz in near:
        send(X.at[0, 0], X.at[0, NZ - dz], z_send, z_recv.at[NZ - dz - 1], at(dz=dz))
    to_x(0)
    partner = at(dc=1)
    for i, (src, dst) in enumerate(weights):
        send(src, dst.at[1], wx_send.at[i], wx_recv.at[i], partner)
    for dz in near:
        wait(X.at[0, dz], z_recv.at[dz - 1])
        to_x(dz)

    low = lax.broadcasted_iota(jnp.int32, (NZ // 2, 8, D), 1) < TB

    def front(j):
        if j:
            wait(X.at[j], x_recv.at[j - 1])
        rows = pl.ds(CT * j, CT)
        v = X[j].astype(F32).reshape(NZ // 2, 2, 8, D)
        even, odd = v[:, 0], v[:, 1]
        t = jnp.where(low, even, pltpu.roll(odd, TB, 1)).reshape(CT, D).astype(BF16)
        g = jnp.where(low, pltpu.roll(even, TB, 1), odd).reshape(CT, D).astype(BF16)
        T[0, rows] = t
        G[0, rows] = g
        send(T.at[0, rows], T.at[1, rows], t_send.at[0], t_recv.at[0], partner)
        send(G.at[0, rows], G.at[1, rows], t_send.at[1], t_recv.at[1], partner)
        for h in range(2):
            if j == 0:
                for i, (src, dst) in enumerate(weights):
                    wait(dst.at[h], (wx_recv if h else w_sem).at[i])
            parts = (dot(t, Wg[h]), dot(t, Wu[h]), dot_nt(g, Wd[h]))
            for half in range(2):
                for c in range(2):
                    q = 4 * half + 2 * h + c
                    for a, part in enumerate(parts):
                        S1[j, q, a] = part[ROWS * half : ROWS * (half + 1), LANES * c : LANES * (c + 1)].astype(BF16)
        for d in (4, 3, 5, 2, 6, 1, 7):
            q = lax.rem(y + d, NY)
            send(S1.at[j, q], R1.at[j, NY - d - 1], y1_send.at[j], y1_recv.at[j], at(dy=d))

    def middle(j):
        wait(R1.at[j], y1_recv.at[j])
        gate, up, back = (
            S1[j, y, a].astype(F32) + jnp.sum(R1[j, :, a].astype(F32), axis=0)
            for a in range(3)
        )
        sig = jax.nn.sigmoid(gate)
        R2[j, y, 0] = (gate * sig * up).astype(BF16)
        R2[j, y, 1] = (back * up * sig * (1.0 + gate * (1.0 - sig))).astype(BF16)
        R2[j, y, 2] = (back * gate * sig).astype(BF16)
        for d in (4, 3, 5, 2, 6, 1, 7):
            send(R2.at[j, y], R2.at[j, y], y2_send.at[j], y2_recv.at[j], at(dy=d))

    def back_end(j):
        wait(R2.at[j, pl.ds(0, NY - 1)], y2_recv.at[j])
        rows = pl.ds(CT * j, CT)
        full = []
        for a in range(3):
            v = jnp.concatenate(
                [
                    jnp.concatenate([R2[j, 4 * half + c, a].astype(F32) for c in range(4)], axis=1)
                    for half in range(2)
                ],
                axis=0,
            ).astype(BF16)
            own, other = v[:, :F], v[:, F:]
            H[0, a, rows] = own
            HP[a, rows] = other
            full.append((own, other))
        for a in range(3):
            send(HP.at[a, rows], H.at[1, a, rows], h_send.at[a], h_recv.at[a], partner)
        (h0, h1), (g0, g1), (u0, u1) = full
        m = (dot(h0, Wd[0]) + dot(h1, Wd[1])).reshape(NZ // 2, 8, D)
        n = (dot_nt(g0, Wg[0]) + dot_nt(g1, Wg[1]) + dot_nt(u0, Wu[0]) + dot_nt(u1, Wu[1])).reshape(NZ // 2, 8, D)
        even = jnp.where(low, m, pltpu.roll(n, TB, 1))
        odd = jnp.where(low, pltpu.roll(m, TB, 1), n)
        for p in range(NZ // 2):
            if j:
                SX[j - 1, 2 * p] = even[p].astype(BF16)
                SX[j - 1, 2 * p + 1] = odd[p].astype(BF16)
            else:
                OX[2 * p] = even[p]
                OX[2 * p + 1] = odd[p]
        if j:
            send(SX.at[j - 1], RX.at[NX - j - 1], rx_send.at[j - 1], rx_recv.at[NX - j - 1], at(dx=j))

    stages = []
    for k in range(len(ORDER) + 4):
        if k < 4:
            front(ORDER[k])
        if 0 <= k - 1 < 4:
            middle(ORDER[k - 1])
        if 0 <= k - 2 < 4:
            back_end(ORDER[k - 2])

    for i in range(2):
        wait(T.at[1], t_recv.at[0]) if i == 0 else wait(G.at[1], t_recv.at[1])
    for a in range(3):
        wait(H.at[1, a], h_recv.at[a])
    for a, (buf, out) in enumerate(((A1, ggate), (A2, gup))):
        buf[...] = (dot_tn(T[0], H[0, a + 1]) + dot_tn(T[1], H[1, a + 1])).astype(BF16)
        pltpu.make_async_copy(buf, out, o_sem.at[a]).start()

    for s in range(NX - 1):
        wait(RX.at[s], rx_recv.at[s])
    for dz in near[::-1]:
        SZ[dz - 1] = (OX[dz] + RX[0, dz].astype(F32) + RX[1, dz].astype(F32) + RX[2, dz].astype(F32)).astype(BF16)
        send(SZ.at[dz - 1], RZ.at[NZ - dz - 1], rz_send, rz_recv, at(dz=dz))
    total = OX[0] + RX[0, 0].astype(F32) + RX[1, 0].astype(F32) + RX[2, 0].astype(F32)

    A3[...] = (dot_tn(H[0, 0], G[0]) + dot_tn(H[1, 0], G[1])).astype(BF16)
    pltpu.make_async_copy(A3, gdown, o_sem.at[2]).start()

    wait(RZ, rz_recv)
    total += jnp.sum(RZ[...].astype(F32), axis=0)
    mixed[...] = total[:TB].astype(BF16)
    gtok[...] = total[TB:].astype(BF16)

    wait(RZ, z_send)
    wait(X.at[pl.ds(0, NX - 1)], x_send)
    wait(RZ, rz_send)
    for i, (src, dst) in enumerate(weights):
        wait(dst.at[0], wx_send.at[i])
    wait(T.at[0], t_send.at[0])
    wait(G.at[0], t_send.at[1])
    for a in range(3):
        wait(HP.at[a], h_send.at[a])
        wait(SX.at[a], rx_send.at[a])
    for j in range(NX):
        wait(R1.at[j], y1_send.at[j])
        wait(R1.at[j], y2_send.at[j])
    for a, (buf, out) in enumerate(((A1, ggate), (A2, gup), (A3, gdown))):
        pltpu.make_async_copy(buf, out, o_sem.at[a]).wait()


def on_device(tokens, grad_out, gate_weight, up_weight, down_weight):
    vmem = pl.BlockSpec(memory_space=pltpu.VMEM)
    hbm = pl.BlockSpec(memory_space=pl.ANY)
    dma = pltpu.SemaphoreType.DMA
    return pl.pallas_call(
        kernel,
        name="ffn",
        out_shape=(
            jax.ShapeDtypeStruct((TB, D), BF16),
            jax.ShapeDtypeStruct((TB, D), BF16),
            jax.ShapeDtypeStruct((D, F), BF16),
            jax.ShapeDtypeStruct((D, F), BF16),
            jax.ShapeDtypeStruct((F, D), BF16),
        ),
        in_specs=[vmem, vmem, hbm, hbm, hbm],
        out_specs=(vmem, vmem, hbm, hbm, hbm),
        scratch_shapes=[
            pltpu.VMEM((NX, NZ, 8, D), BF16),
            pltpu.VMEM((2, D, F), BF16),
            pltpu.VMEM((2, D, F), BF16),
            pltpu.VMEM((2, F, D), BF16),
            pltpu.VMEM((2, NX * CT, D), BF16),
            pltpu.VMEM((2, NX * CT, D), BF16),
            pltpu.VMEM((NX, NY, 3, ROWS, LANES), BF16),
            pltpu.VMEM((NX, NY - 1, 3, ROWS, LANES), BF16),
            pltpu.VMEM((NX, NY, 3, ROWS, LANES), BF16),
            pltpu.VMEM((2, 3, NX * CT, F), BF16),
            pltpu.VMEM((3, NX * CT, F), BF16),
            pltpu.VMEM((NX - 1, NZ, 8, D), BF16),
            pltpu.VMEM((NX - 1, NZ, 8, D), BF16),
            pltpu.VMEM((NZ, 8, D), F32),
            pltpu.VMEM((NZ - 1, 8, D), BF16),
            pltpu.VMEM((NZ - 1, 8, D), BF16),
            pltpu.VMEM((D, F), BF16),
            pltpu.VMEM((D, F), BF16),
            pltpu.VMEM((F, D), BF16),
            dma((3,)),
            dma((3,)),
            dma((3,)),
            dma,
            dma((NZ - 1,)),
            dma,
            dma((NX - 1,)),
            dma((2,)),
            dma((2,)),
            dma((NX,)),
            dma((NX,)),
            dma((NX,)),
            dma((NX,)),
            dma((3,)),
            dma((3,)),
            dma((3,)),
            dma((3,)),
            dma,
            dma,
            dma((3,)),
        ],
        compiler_params=pltpu.CompilerParams(
            collective_id=0, has_side_effects=True, vmem_limit_bytes=40 * 2**20
        ),
        cost_estimate=pl.CostEstimate(
            flops=18 * 384 * D * F, bytes_accessed=2**23, transcendentals=2**17
        ),
    )(tokens, grad_out, gate_weight, up_weight, down_weight)


def solution(mesh):
    by_token = P(("inner", "out"), "row")
    by_hidden = P("row", ("inner", "out"))
    return jax.shard_map(
        on_device,
        mesh=mesh,
        in_specs=(by_token, by_token, by_hidden, by_hidden, by_token),
        out_specs=(by_token, by_token, by_hidden, by_hidden, by_token),
        check_vma=False,
    )
```

```python
import functools

import jax
import jax.numpy as jnp
from jax import lax
from jax.experimental import pallas as pl
from jax.experimental.pallas import tpu as pltpu
from jax.sharding import PartitionSpec as P

MESH = pl.DeviceIdType.MESH
BF16, F32 = jnp.bfloat16, jnp.float32

NX, NY, NZ = 4, 8, 12
Z_LO = 6
TB = 4
D = 1024
F = 256
CT = NZ * TB
ROWS, LANES = CT // 2, 128
KNEE4, KNEE2 = 2.0**-12, 2.0**-30
ORDER = (0, 1, 3, 2)


def dot(a, b):
    return jnp.dot(a, b, preferred_element_type=F32)


def dot_nt(a, b):
    return lax.dot_general(a, b, (((1,), (1,)), ((), ())), preferred_element_type=F32)


def dot_tn(a, b):
    return lax.dot_general(a, b, (((0,), (0,)), ((), ())), preferred_element_type=F32)


def coded4(v):
    r = jnp.maximum(jnp.abs(v) * (1.0 / KNEE4), 1.0)
    return (v * (r * r * r)).astype(BF16)


def decoded4(c):
    c = c.astype(F32)
    root = lax.rsqrt(jnp.maximum(jnp.abs(c) * (1.0 / KNEE4), 1.0))
    return c * (root * jnp.sqrt(root))


def coded2(v):
    return (v * jnp.maximum(jnp.abs(v) * (1.0 / KNEE2), 1.0)).astype(BF16)


def decoded2(c):
    c = c.astype(F32)
    return c * lax.rsqrt(jnp.maximum(jnp.abs(c) * (1.0 / KNEE2), 1.0))


def kernel(
    tok_in, gout_in, wg_in, wu_in, wd_in,
    mixed, gtok, ggate, gup, gdown,
    tok, gout, X, Wg, Wu, Wd, T, G, S1, R1, R2, H, HP, SX, RX, OX, SZ, RZ, A1, A2, A3,
    in_sem, w_sem, wx_send, wx_recv, z_send, z_recv, x_send, x_recv, t_send, t_recv,
    y1_send, y1_recv, y2_send, y2_recv, h_send, h_recv,
    rx_send, rx_recv, rz_send, rz_recv, o_sem,
):
    y = lax.axis_index("row")
    z = lax.axis_index("inner")
    o = lax.axis_index("out")
    core = lax.rem(o, 2)
    x = lax.rem(o // 2, NX)
    z = z + Z_LO * (o // (2 * NX))

    def at(dx=0, dy=0, dz=0, dc=0):
        xx = lax.rem(x + dx, NX)
        zz = lax.rem(z + dz, NZ)
        cc = lax.rem(core + dc, 2)
        return (
            lax.rem(y + dy, NY),
            lax.rem(zz, Z_LO),
            ((zz // Z_LO) * NX + xx) * 2 + cc,
        )

    def send(src, dst, ssem, rsem, to):
        copy = pltpu.make_async_remote_copy(
            src_ref=src, dst_ref=dst, send_sem=ssem, recv_sem=rsem,
            device_id=to, device_id_type=MESH,
        )
        copy.start()

    def wait(ref, sem):
        pltpu.make_async_copy(ref, ref, sem).wait()

    pltpu.make_async_copy(tok_in, tok, in_sem.at[0]).start()
    pltpu.make_async_copy(gout_in, gout, in_sem.at[1]).start()
    barrier = pltpu.get_barrier_semaphore()
    peers = (
        [at(dz=d) for d in range(1, NZ)]
        + [at(dx=d) for d in range(1, NX)]
        + [at(dy=d) for d in range(1, NY)]
        + [at(dc=1)]
    )
    for peer in peers:
        pl.semaphore_signal(barrier, inc=1, device_id=peer, device_id_type=MESH)

    weights = ((wg_in, Wg), (wu_in, Wu), (wd_in, Wd))
    for i, (src, dst) in enumerate(weights):
        pltpu.make_async_copy(src, dst.at[0], w_sem.at[i]).start()

    pltpu.make_async_copy(tok_in, tok, in_sem.at[0]).wait()
    pltpu.make_async_copy(gout_in, gout, in_sem.at[1]).wait()
    X[0, 0] = jnp.concatenate([tok[...].astype(F32), gout[...].astype(F32)], axis=0).astype(BF16)

    pl.semaphore_wait(barrier, len(peers))

    near = [1, 11, 2, 10, 3, 9, 4, 8, 5, 7, 6]

    def to_x(dz):
        for dx in (1, 3, 2):
            send(X.at[0, dz], X.at[NX - dx, dz], x_send, x_recv.at[NX - dx - 1], at(dx=dx))

    for dz in near:
        send(X.at[0, 0], X.at[0, NZ - dz], z_send, z_recv.at[NZ - dz - 1], at(dz=dz))
    to_x(0)
    partner = at(dc=1)
    for i, (src, dst) in enumerate(weights):
        send(src, dst.at[1], wx_send.at[i], wx_recv.at[i], partner)
    for dz in near:
        wait(X.at[0, dz], z_recv.at[dz - 1])
        to_x(dz)

    low = lax.broadcasted_iota(jnp.int32, (NZ // 2, 8, D), 1) < TB

    def front(j):
        if j:
            wait(X.at[j], x_recv.at[j - 1])
        rows = pl.ds(CT * j, CT)
        v = X[j].astype(F32).reshape(NZ // 2, 2, 8, D)
        even, odd = v[:, 0], v[:, 1]
        t = jnp.where(low, even, pltpu.roll(odd, TB, 1)).reshape(CT, D).astype(BF16)
        g = jnp.where(low, pltpu.roll(even, TB, 1), odd).reshape(CT, D).astype(BF16)
        T[0, rows] = t
        G[0, rows] = g
        send(T.at[0, rows], T.at[1, rows], t_send.at[0], t_recv.at[0], partner)
        send(G.at[0, rows], G.at[1, rows], t_send.at[1], t_recv.at[1], partner)
        for h in range(2):
            if j == 0:
                for i, (src, dst) in enumerate(weights):
                    wait(dst.at[h], (wx_recv if h else w_sem).at[i])
            parts = (dot(t, Wg[h]), dot(t, Wu[h]), dot_nt(g, Wd[h]))
            for half in range(2):
                for c in range(2):
                    q = 4 * half + 2 * h + c
                    for a, part in enumerate(parts):
                        S1[j, q, a] = coded4(
                            part[ROWS * half : ROWS * (half + 1), LANES * c : LANES * (c + 1)]
                        )
        for d in (4, 3, 5, 2, 6, 1, 7):
            q = lax.rem(y + d, NY)
            send(S1.at[j, q], R1.at[j, NY - d - 1], y1_send.at[j], y1_recv.at[j], at(dy=d))

    def middle(j):
        wait(R1.at[j], y1_recv.at[j])
        gate, up, back = (
            decoded4(S1[j, y, a]) + jnp.sum(decoded4(R1[j, :, a]), axis=0)
            for a in range(3)
        )
        sig = jax.nn.sigmoid(gate)
        R2[j, y, 0] = (gate * sig * up).astype(BF16)
        R2[j, y, 1] = (back * up * sig * (1.0 + gate * (1.0 - sig))).astype(BF16)
        R2[j, y, 2] = (back * gate * sig).astype(BF16)
        for d in (4, 3, 5, 2, 6, 1, 7):
            send(R2.at[j, y], R2.at[j, y], y2_send.at[j], y2_recv.at[j], at(dy=d))

    def back_end(j):
        wait(R2.at[j, pl.ds(0, NY - 1)], y2_recv.at[j])
        rows = pl.ds(CT * j, CT)
        full = []
        for a in range(3):
            v = jnp.concatenate(
                [
                    jnp.concatenate([R2[j, 4 * half + c, a].astype(F32) for c in range(4)], axis=1)
                    for half in range(2)
                ],
                axis=0,
            ).astype(BF16)
            own, other = v[:, :F], v[:, F:]
            H[0, a, rows] = own
            HP[a, rows] = other
            full.append((own, other))
        for a in range(3):
            send(HP.at[a, rows], H.at[1, a, rows], h_send.at[a], h_recv.at[a], partner)
        (h0, h1), (g0, g1), (u0, u1) = full
        m = (dot(h0, Wd[0]) + dot(h1, Wd[1])).reshape(NZ // 2, 8, D)
        n = (dot_nt(g0, Wg[0]) + dot_nt(g1, Wg[1]) + dot_nt(u0, Wu[0]) + dot_nt(u1, Wu[1])).reshape(NZ // 2, 8, D)
        even = jnp.where(low, m, pltpu.roll(n, TB, 1))
        odd = jnp.where(low, pltpu.roll(m, TB, 1), n)
        for p in range(NZ // 2):
            if j:
                SX[j - 1, 2 * p] = coded2(even[p])
                SX[j - 1, 2 * p + 1] = coded2(odd[p])
            else:
                OX[2 * p] = even[p]
                OX[2 * p + 1] = odd[p]
        if j:
            send(SX.at[j - 1], RX.at[NX - j - 1], rx_send.at[j - 1], rx_recv.at[NX - j - 1], at(dx=j))

    stages = []
    for k in range(len(ORDER) + 4):
        if k < 4:
            front(ORDER[k])
        if 0 <= k - 1 < 4:
            middle(ORDER[k - 1])
        if 0 <= k - 2 < 4:
            back_end(ORDER[k - 2])

    for i in range(2):
        wait(T.at[1], t_recv.at[0]) if i == 0 else wait(G.at[1], t_recv.at[1])
    for a in range(3):
        wait(H.at[1, a], h_recv.at[a])
    for a, (buf, out) in enumerate(((A1, ggate), (A2, gup))):
        buf[...] = (dot_tn(T[0], H[0, a + 1]) + dot_tn(T[1], H[1, a + 1])).astype(BF16)
        pltpu.make_async_copy(buf, out, o_sem.at[a]).start()

    for s in range(NX - 1):
        wait(RX.at[s], rx_recv.at[s])
    for dz in near[::-1]:
        SZ[dz - 1] = coded2(OX[dz] + jnp.sum(decoded2(RX[:, dz]), axis=0))
        send(SZ.at[dz - 1], RZ.at[NZ - dz - 1], rz_send, rz_recv, at(dz=dz))
    total = OX[0] + jnp.sum(decoded2(RX[:, 0]), axis=0)

    A3[...] = (dot_tn(H[0, 0], G[0]) + dot_tn(H[1, 0], G[1])).astype(BF16)
    pltpu.make_async_copy(A3, gdown, o_sem.at[2]).start()

    wait(RZ, rz_recv)
    total += jnp.sum(decoded2(RZ[...]), axis=0)
    tok[...] = total[:TB].astype(BF16)
    gout[...] = total[TB:].astype(BF16)
    pltpu.make_async_copy(tok, mixed, o_sem.at[3]).start()
    pltpu.make_async_copy(gout, gtok, o_sem.at[4]).start()

    wait(RZ, z_send)
    wait(X.at[pl.ds(0, NX - 1)], x_send)
    wait(RZ, rz_send)
    for i, (src, dst) in enumerate(weights):
        wait(dst.at[0], wx_send.at[i])
    wait(T.at[0], t_send.at[0])
    wait(G.at[0], t_send.at[1])
    for a in range(3):
        wait(HP.at[a], h_send.at[a])
        wait(SX.at[a], rx_send.at[a])
    for j in range(NX):
        wait(R1.at[j], y1_send.at[j])
        wait(R1.at[j], y2_send.at[j])
    for a, (buf, out) in enumerate(((A1, ggate), (A2, gup), (A3, gdown), (tok, mixed), (gout, gtok))):
        pltpu.make_async_copy(buf, out, o_sem.at[a]).wait()


PIECES = 4


def store(*refs):
    *pairs, sem = refs
    n = len(pairs) // 2
    copies = []
    for i, (src, dst) in enumerate(zip(pairs[:n], pairs[n:])):
        rows = src.shape[0] // PIECES if src.shape[0] > TB else TB
        for k in range(src.shape[0] // rows):
            part = pl.ds(k * rows, rows)
            copies.append(pltpu.make_async_copy(src.at[part], dst.at[part], sem.at[i * PIECES + k]))
    for copy in copies:
        copy.start()
    for copy in copies:
        copy.wait()


def on_device(tokens, grad_out, gate_weight, up_weight, down_weight):
    vmem = pl.BlockSpec(memory_space=pltpu.VMEM)
    hbm = pl.BlockSpec(memory_space=pltpu.HBM)
    dma = pltpu.SemaphoreType.DMA
    out_shape = tuple(
        jax.ShapeDtypeStruct(shape, BF16) for shape in ((TB, D), (TB, D), (D, F), (D, F), (F, D))
    )
    outs = pl.pallas_call(
        kernel,
        name="ffn",
        out_shape=out_shape,
        in_specs=[hbm, hbm, hbm, hbm, hbm],
        out_specs=(hbm,) * 5,
        scratch_shapes=[
            pltpu.VMEM((TB, D), BF16),
            pltpu.VMEM((TB, D), BF16),
            pltpu.VMEM((NX, NZ, 8, D), BF16),
            pltpu.VMEM((2, D, F), BF16),
            pltpu.VMEM((2, D, F), BF16),
            pltpu.VMEM((2, F, D), BF16),
            pltpu.VMEM((2, NX * CT, D), BF16),
            pltpu.VMEM((2, NX * CT, D), BF16),
            pltpu.VMEM((NX, NY, 3, ROWS, LANES), BF16),
            pltpu.VMEM((NX, NY - 1, 3, ROWS, LANES), BF16),
            pltpu.VMEM((NX, NY, 3, ROWS, LANES), BF16),
            pltpu.VMEM((2, 3, NX * CT, F), BF16),
            pltpu.VMEM((3, NX * CT, F), BF16),
            pltpu.VMEM((NX - 1, NZ, 8, D), BF16),
            pltpu.VMEM((NX - 1, NZ, 8, D), BF16),
            pltpu.VMEM((NZ, 8, D), F32),
            pltpu.VMEM((NZ - 1, 8, D), BF16),
            pltpu.VMEM((NZ - 1, 8, D), BF16),
            pltpu.VMEM((D, F), BF16),
            pltpu.VMEM((D, F), BF16),
            pltpu.VMEM((F, D), BF16),
            dma((2,)),
            dma((3,)),
            dma((3,)),
            dma((3,)),
            dma,
            dma((NZ - 1,)),
            dma,
            dma((NX - 1,)),
            dma((2,)),
            dma((2,)),
            dma((NX,)),
            dma((NX,)),
            dma((NX,)),
            dma((NX,)),
            dma((3,)),
            dma((3,)),
            dma((3,)),
            dma((3,)),
            dma,
            dma,
            dma((5,)),
        ],
        compiler_params=pltpu.CompilerParams(
            collective_id=0, has_side_effects=True, vmem_limit_bytes=62 * 2**20
        ),
        cost_estimate=pl.CostEstimate(
            flops=18 * 384 * D * F, bytes_accessed=2**23, transcendentals=2**17
        ),
    )(tokens, grad_out, gate_weight, up_weight, down_weight)
    return pl.pallas_call(
        store,
        name="store",
        out_shape=out_shape,
        in_specs=[hbm] * 5,
        out_specs=(hbm,) * 5,
        scratch_shapes=[dma((5 * PIECES,))],
        compiler_params=pltpu.CompilerParams(vmem_limit_bytes=62 * 2**20),
    )(*outs)


def solution(mesh):
    by_token = P(("inner", "out"), "row")
    by_hidden = P("row", ("inner", "out"))
    return jax.shard_map(
        on_device,
        mesh=mesh,
        in_specs=(by_token, by_token, by_hidden, by_hidden, by_token),
        out_specs=(by_token, by_token, by_hidden, by_hidden, by_token),
        check_vma=False,
    )
```

```python
import functools

import jax
import jax.numpy as jnp
from jax import lax
from jax.experimental import pallas as pl
from jax.experimental.pallas import tpu as pltpu
from jax.sharding import PartitionSpec as P

MESH = pl.DeviceIdType.MESH
BF16, F32 = jnp.bfloat16, jnp.float32

NX, NY, NZ = 4, 8, 12
Z_LO = 6
TB = 4
D = 1024
F = 256
CT = NZ * TB
ROWS, LANES = CT // 2, 128
KNEE4, KNEE2 = 2.0**-12, 2.0**-30
FRONT = (0, 2, 1, 3)
BACK = (2, 1, 3, 0)


def dot(a, b):
    return jnp.dot(a, b, preferred_element_type=F32)


def dot_nt(a, b):
    return lax.dot_general(a, b, (((1,), (1,)), ((), ())), preferred_element_type=F32)


def dot_tn(a, b):
    return lax.dot_general(a, b, (((0,), (0,)), ((), ())), preferred_element_type=F32)


def coded4(v):
    r = jnp.maximum(jnp.abs(v) * (1.0 / KNEE4), 1.0)
    return (v * (r * r * r)).astype(BF16)


def decoded4(c):
    c = c.astype(F32)
    root = lax.rsqrt(jnp.maximum(jnp.abs(c) * (1.0 / KNEE4), 1.0))
    return c * (root * jnp.sqrt(root))


def coded2(v):
    return (v * jnp.maximum(jnp.abs(v) * (1.0 / KNEE2), 1.0)).astype(BF16)


def decoded2(c):
    c = c.astype(F32)
    return c * lax.rsqrt(jnp.maximum(jnp.abs(c) * (1.0 / KNEE2), 1.0))


def kernel(
    tok_in, gout_in, wg_in, wu_in, wd_in,
    mixed, gtok, ggate, gup, gdown,
    tok, gout, X, Wg, Wu, Wd, T, G, S1, K1, S2, R1, R2, H, HP, SX, RX, OX, SZ, RZ, A1, A2, A3,
    in_sem, w_sem, wx_send, wx_recv, z_send, z_recv, x_send, x_recv, t_send, t_recv,
    k1_recv, y1_send, y1_recv, y2_send, k2_recv, y2_recv, h_send, h_recv,
    rx_send, rx_recv, rz_send, rz_recv, o_sem,
):
    y = lax.axis_index("row")
    z = lax.axis_index("inner")
    o = lax.axis_index("out")
    core = lax.rem(o, 2)
    x = lax.rem(o // 2, NX)
    z = z + Z_LO * (o // (2 * NX))

    def at(dx=0, dy=0, dz=0, dc=0):
        xx = lax.rem(x + dx, NX)
        zz = lax.rem(z + dz, NZ)
        cc = lax.rem(core + dc, 2)
        return (
            lax.rem(y + dy, NY),
            lax.rem(zz, Z_LO),
            ((zz // Z_LO) * NX + xx) * 2 + cc,
        )

    def send(src, dst, ssem, rsem, to):
        copy = pltpu.make_async_remote_copy(
            src_ref=src, dst_ref=dst, send_sem=ssem, recv_sem=rsem,
            device_id=to, device_id_type=MESH,
        )
        copy.start()

    def wait(ref, sem):
        pltpu.make_async_copy(ref, ref, sem).wait()

    pltpu.make_async_copy(tok_in, tok, in_sem.at[0]).start()
    pltpu.make_async_copy(gout_in, gout, in_sem.at[1]).start()
    barrier = pltpu.get_barrier_semaphore()
    peers = (
        [at(dz=d) for d in range(1, NZ)]
        + [at(dx=d) for d in range(1, NX)]
        + [at(dy=d) for d in (1, 2, NY - 2, NY - 1)]
        + [at(dc=1)]
    )
    for peer in peers:
        pl.semaphore_signal(barrier, inc=1, device_id=peer, device_id_type=MESH)

    weights = ((wg_in, Wg), (wu_in, Wu), (wd_in, Wd))
    for i, (src, dst) in enumerate(weights):
        pltpu.make_async_copy(src, dst.at[0], w_sem.at[i]).start()

    pltpu.make_async_copy(tok_in, tok, in_sem.at[0]).wait()
    pltpu.make_async_copy(gout_in, gout, in_sem.at[1]).wait()
    X[0, 0] = jnp.concatenate([tok[...].astype(F32), gout[...].astype(F32)], axis=0).astype(BF16)

    pl.semaphore_wait(barrier, len(peers))

    near = [1, 11, 2, 10, 3, 9, 4, 8, 5, 7, 6]

    def to_x(dz):
        for dx in (2, 1, 3):
            send(X.at[0, dz], X.at[NX - dx, dz], x_send, x_recv.at[NX - dx - 1], at(dx=dx))

    for dz in near:
        send(X.at[0, 0], X.at[0, NZ - dz], z_send, z_recv.at[NZ - dz - 1], at(dz=dz))
    to_x(0)
    partner = at(dc=1)
    for i, (src, dst) in enumerate(weights):
        send(src, dst.at[1], wx_send.at[i], wx_recv.at[i], partner)
    for dz in near:
        wait(X.at[0, dz], z_recv.at[dz - 1])
        to_x(dz)

    low = lax.broadcasted_iota(jnp.int32, (NZ // 2, 8, D), 1) < TB

    def front(j):
        if j:
            wait(X.at[j], x_recv.at[j - 1])
        rows = pl.ds(CT * j, CT)
        v = X[j].astype(F32).reshape(NZ // 2, 2, 8, D)
        even, odd = v[:, 0], v[:, 1]
        t = jnp.where(low, even, pltpu.roll(odd, TB, 1)).reshape(CT, D).astype(BF16)
        g = jnp.where(low, pltpu.roll(even, TB, 1), odd).reshape(CT, D).astype(BF16)
        T[0, rows] = t
        G[0, rows] = g
        send(T.at[0, rows], T.at[1, rows], t_send.at[0], t_recv.at[0], partner)
        send(G.at[0, rows], G.at[1, rows], t_send.at[1], t_recv.at[1], partner)
        for h in range(2):
            if j == 0:
                for i, (src, dst) in enumerate(weights):
                    wait(dst.at[h], (wx_recv if h else w_sem).at[i])
            parts = (dot(t, Wg[h]), dot(t, Wu[h]), dot_nt(g, Wd[h]))
            for half in range(2):
                for c in range(2):
                    q = 4 * half + 2 * h + c
                    for a, part in enumerate(parts):
                        S1[j, q, a] = coded4(
                            part[ROWS * half : ROWS * (half + 1), LANES * c : LANES * (c + 1)]
                        )
        via = 2 if j % 2 == 0 else -2
        for to, q, dst, sem in (
            (via, 4, K1.at[j, 2], k1_recv),
            (1, 3, K1.at[j, 0], k1_recv),
            (-1, -3, K1.at[j, 1], k1_recv),
            (1, 1, R1.at[j, 0], y1_recv),
            (-1, -1, R1.at[j, 1], y1_recv),
        ):
            send(S1.at[j, around(q)], dst, y1_send.at[j], sem.at[j], at(dy=to % NY))

    def around(d):
        return lax.rem(y + d % NY, NY)

    def relay(j):
        wait(K1.at[j], k1_recv.at[j])
        for i, to in enumerate((2, -2)):
            v = decoded4(S1[j, around(to)]) + decoded4(K1[j, i])
            if i == j % 2:
                v += decoded4(K1[j, 2])
            S2[j, i] = coded4(v)
            send(S2.at[j, i], R1.at[j, 2 + i], y1_send.at[j], y1_recv.at[j], at(dy=to % NY))

    def middle(j):
        wait(R1.at[j], y1_recv.at[j])
        gate, up, back = (
            decoded4(S1[j, y, a]) + jnp.sum(decoded4(R1[j, :, a]), axis=0)
            for a in range(3)
        )
        sig = jax.nn.sigmoid(gate)
        R2[j, y, 0] = (gate * sig * up).astype(BF16)
        R2[j, y, 1] = (back * up * sig * (1.0 + gate * (1.0 - sig))).astype(BF16)
        R2[j, y, 2] = (back * gate * sig).astype(BF16)
        for to, sem in ((2, k2_recv), (-2, k2_recv), (1, y2_recv), (-1, y2_recv)):
            send(R2.at[j, y], R2.at[j, y], y2_send.at[j], sem.at[j], at(dy=to % NY))

    def spread(j):
        wait(R2.at[j, pl.ds(0, 2)], k2_recv.at[j])
        via = 2 if j % 2 == 0 else -2
        for to, q in ((via, -via), (1, -2), (-1, 2)):
            block = R2.at[j, around(q)]
            send(block, block, y2_send.at[j], y2_recv.at[j], at(dy=to % NY))

    def back_end(j):
        wait(R2.at[j, pl.ds(0, NY - 3)], y2_recv.at[j])
        rows = pl.ds(CT * j, CT)
        full = []
        for a in range(3):
            v = jnp.concatenate(
                [
                    jnp.concatenate([R2[j, 4 * half + c, a].astype(F32) for c in range(4)], axis=1)
                    for half in range(2)
                ],
                axis=0,
            ).astype(BF16)
            own, other = v[:, :F], v[:, F:]
            H[0, a, rows] = own
            HP[a, rows] = other
            full.append((own, other))
        for a in range(3):
            send(HP.at[a, rows], H.at[1, a, rows], h_send.at[a], h_recv.at[a], partner)
        (h0, h1), (g0, g1), (u0, u1) = full
        m = (dot(h0, Wd[0]) + dot(h1, Wd[1])).reshape(NZ // 2, 8, D)
        n = (dot_nt(g0, Wg[0]) + dot_nt(g1, Wg[1]) + dot_nt(u0, Wu[0]) + dot_nt(u1, Wu[1])).reshape(NZ // 2, 8, D)
        even = jnp.where(low, m, pltpu.roll(n, TB, 1))
        odd = jnp.where(low, pltpu.roll(m, TB, 1), n)
        for p in range(NZ // 2):
            if j:
                SX[j - 1, 2 * p] = coded2(even[p])
                SX[j - 1, 2 * p + 1] = coded2(odd[p])
            else:
                OX[2 * p] = even[p]
                OX[2 * p + 1] = odd[p]
        if j:
            send(SX.at[j - 1], RX.at[NX - j - 1], rx_send.at[j - 1], rx_recv.at[NX - j - 1], at(dx=j))

    f, b = FRONT, BACK
    front(f[0])
    front(f[1])
    relay(f[0])
    front(f[2])
    relay(f[1])
    front(f[3])
    relay(f[2])
    middle(b[0])
    relay(f[3])
    middle(b[1])
    spread(b[0])
    middle(b[2])
    spread(b[1])
    back_end(b[0])
    middle(b[3])
    spread(b[2])
    back_end(b[1])
    spread(b[3])
    back_end(b[2])
    back_end(b[3])

    for i in range(2):
        wait(T.at[1], t_recv.at[0]) if i == 0 else wait(G.at[1], t_recv.at[1])
    for a in range(3):
        wait(H.at[1, a], h_recv.at[a])
    for a, (buf, out) in enumerate(((A1, ggate), (A2, gup))):
        buf[...] = (dot_tn(T[0], H[0, a + 1]) + dot_tn(T[1], H[1, a + 1])).astype(BF16)
        pltpu.make_async_copy(buf, out, o_sem.at[a]).start()

    for s in range(NX - 1):
        wait(RX.at[s], rx_recv.at[s])
    for dz in near[::-1]:
        SZ[dz - 1] = coded2(OX[dz] + jnp.sum(decoded2(RX[:, dz]), axis=0))
        send(SZ.at[dz - 1], RZ.at[NZ - dz - 1], rz_send, rz_recv, at(dz=dz))
    total = OX[0] + jnp.sum(decoded2(RX[:, 0]), axis=0)

    A3[...] = (dot_tn(H[0, 0], G[0]) + dot_tn(H[1, 0], G[1])).astype(BF16)
    pltpu.make_async_copy(A3, gdown, o_sem.at[2]).start()

    wait(RZ, rz_recv)
    total += jnp.sum(decoded2(RZ[...]), axis=0)
    tok[...] = total[:TB].astype(BF16)
    gout[...] = total[TB:].astype(BF16)
    pltpu.make_async_copy(tok, mixed, o_sem.at[3]).start()
    pltpu.make_async_copy(gout, gtok, o_sem.at[4]).start()

    wait(RZ, z_send)
    wait(X.at[pl.ds(0, NX - 1)], x_send)
    wait(RZ, rz_send)
    for i, (src, dst) in enumerate(weights):
        wait(dst.at[0], wx_send.at[i])
    wait(T.at[0], t_send.at[0])
    wait(G.at[0], t_send.at[1])
    for a in range(3):
        wait(HP.at[a], h_send.at[a])
        wait(SX.at[a], rx_send.at[a])
    for j in range(NX):
        wait(R2.at[j, pl.ds(0, 7)], y1_send.at[j])
        wait(R2.at[j, pl.ds(0, 7)], y2_send.at[j])
    for a, (buf, out) in enumerate(((A1, ggate), (A2, gup), (A3, gdown), (tok, mixed), (gout, gtok))):
        pltpu.make_async_copy(buf, out, o_sem.at[a]).wait()


def store(*refs):
    n = (len(refs) - 2) // 3
    src, dst, held, (read, write) = refs[:n], refs[n : 2 * n], refs[2 * n : 3 * n], refs[3 * n :]
    for i in range(n):
        pltpu.make_async_copy(src[i], held[i], read.at[i]).start()
    for i in range(n):
        pltpu.make_async_copy(src[i], held[i], read.at[i]).wait()
        pltpu.make_async_copy(held[i], dst[i], write.at[i]).start()
    for i in range(n):
        pltpu.make_async_copy(held[i], dst[i], write.at[i]).wait()


def on_device(tokens, grad_out, gate_weight, up_weight, down_weight):
    vmem = pl.BlockSpec(memory_space=pltpu.VMEM)
    hbm = pl.BlockSpec(memory_space=pltpu.HBM)
    dma = pltpu.SemaphoreType.DMA
    out_shape = tuple(
        jax.ShapeDtypeStruct(shape, BF16) for shape in ((TB, D), (TB, D), (D, F), (D, F), (F, D))
    )
    outs = pl.pallas_call(
        kernel,
        name="ffn",
        out_shape=out_shape,
        in_specs=[hbm, hbm, hbm, hbm, hbm],
        out_specs=(hbm,) * 5,
        scratch_shapes=[
            pltpu.VMEM((TB, D), BF16),
            pltpu.VMEM((TB, D), BF16),
            pltpu.VMEM((NX, NZ, 8, D), BF16),
            pltpu.VMEM((2, D, F), BF16),
            pltpu.VMEM((2, D, F), BF16),
            pltpu.VMEM((2, F, D), BF16),
            pltpu.VMEM((2, NX * CT, D), BF16),
            pltpu.VMEM((2, NX * CT, D), BF16),
            pltpu.VMEM((NX, NY, 3, ROWS, LANES), BF16),
            pltpu.VMEM((NX, 3, 3, ROWS, LANES), BF16),
            pltpu.VMEM((NX, 2, 3, ROWS, LANES), BF16),
            pltpu.VMEM((NX, 4, 3, ROWS, LANES), BF16),
            pltpu.VMEM((NX, NY, 3, ROWS, LANES), BF16),
            pltpu.VMEM((2, 3, NX * CT, F), BF16),
            pltpu.VMEM((3, NX * CT, F), BF16),
            pltpu.VMEM((NX - 1, NZ, 8, D), BF16),
            pltpu.VMEM((NX - 1, NZ, 8, D), BF16),
            pltpu.VMEM((NZ, 8, D), F32),
            pltpu.VMEM((NZ - 1, 8, D), BF16),
            pltpu.VMEM((NZ - 1, 8, D), BF16),
            pltpu.VMEM((D, F), BF16),
            pltpu.VMEM((D, F), BF16),
            pltpu.VMEM((F, D), BF16),
            dma((2,)),
            dma((3,)),
            dma((3,)),
            dma((3,)),
            dma,
            dma((NZ - 1,)),
            dma,
            dma((NX - 1,)),
            dma((2,)),
            dma((2,)),
            dma((NX,)),
            dma((NX,)),
            dma((NX,)),
            dma((NX,)),
            dma((NX,)),
            dma((NX,)),
            dma((3,)),
            dma((3,)),
            dma((3,)),
            dma((3,)),
            dma,
            dma,
            dma((5,)),
        ],
        compiler_params=pltpu.CompilerParams(
            collective_id=0, has_side_effects=True, vmem_limit_bytes=62 * 2**20
        ),
        cost_estimate=pl.CostEstimate(
            flops=18 * 384 * D * F, bytes_accessed=2**23, transcendentals=2**17
        ),
    )(tokens, grad_out, gate_weight, up_weight, down_weight)
    return pl.pallas_call(
        store,
        name="store",
        out_shape=out_shape,
        in_specs=[hbm] * 5,
        out_specs=(hbm,) * 5,
        scratch_shapes=[pltpu.VMEM(o.shape, o.dtype) for o in out_shape] + [dma((5,)), dma((5,))],
        compiler_params=pltpu.CompilerParams(vmem_limit_bytes=62 * 2**20),
    )(*outs)


def solution(mesh):
    by_token = P(("inner", "out"), "row")
    by_hidden = P("row", ("inner", "out"))
    return jax.shard_map(
        on_device,
        mesh=mesh,
        in_specs=(by_token, by_token, by_hidden, by_hidden, by_token),
        out_specs=(by_token, by_token, by_hidden, by_hidden, by_token),
        check_vma=False,
    )
```

```python
import functools

import jax
import jax.numpy as jnp
from jax import lax
from jax.experimental import pallas as pl
from jax.experimental.pallas import tpu as pltpu
from jax.sharding import PartitionSpec as P

MESH = pl.DeviceIdType.MESH
BF16, F32 = jnp.bfloat16, jnp.float32

NX, NY, NZ = 4, 8, 12
Z_LO = 6
TB = 4
D = 1024
F = 256
CT = NZ * TB
ROWS, LANES = CT // 2, 128
KNEE4, KNEE2 = 2.0**-12, 2.0**-30
NC, NG = 4, NZ // 4
Z_ORDER = (0, 1, 11, 6, 5, 7, 4, 8, 3, 9, 2, 10)
Z_SENDS = tuple(NZ - dz for dz in Z_ORDER if dz)
SCHEDULE = (
    ("pass_on", 0, 1, 2, 3),
    ("front", 0, 1, 2, 3),
    ("relay", 0, 1, 2, 3),
    ("turn", 0),
    ("middle", 0, 1, 2, 3),
    ("turn", 1),
    ("spread", 0, 1, 2, 3),
    ("back_end", 0, 1, 2, 3),
    ("finish", 0, 1, 2, 3),
    ("weight_grad", 0, 1, 2),
)
NEAR1 = ()
NEAR2 = ()


def dot(a, b):
    return jnp.dot(a, b, preferred_element_type=F32)


def dot_nt(a, b):
    return lax.dot_general(a, b, (((1,), (1,)), ((), ())), preferred_element_type=F32)


def dot_tn(a, b):
    return lax.dot_general(a, b, (((0,), (0,)), ((), ())), preferred_element_type=F32)


def coded4(v):
    r = jnp.maximum(jnp.abs(v) * (1.0 / KNEE4), 1.0)
    return (v * (r * r * r)).astype(BF16)


def decoded4(c):
    c = c.astype(F32)
    root = lax.rsqrt(jnp.maximum(jnp.abs(c) * (1.0 / KNEE4), 1.0))
    return c * (root * jnp.sqrt(root))


def coded2(v):
    return (v * jnp.maximum(jnp.abs(v) * (1.0 / KNEE2), 1.0)).astype(BF16)


def decoded2(c):
    c = c.astype(F32)
    return c * lax.rsqrt(jnp.maximum(jnp.abs(c) * (1.0 / KNEE2), 1.0))


def kernel(
    tok_in, gout_in, wg_in, wu_in, wd_in,
    mixed, gtok, ggate, gup, gdown,
    tok, gout, X, Wg, Wu, Wd, T, G, TT, S1, K1, S2, R1, R2, H, HP, SX, RX, OX, OZ, SZ, RZ, A1, A2, A3,
    in_sem, w_sem, wx_send, wx_recv, z_send, z_recv, x_send, x_recv, t_send, t_recv,
    k1_recv, y1_send, y1_recv, y2_send, k2_recv, y2_recv, h_send, h_recv,
    rx_send, rx_recv, rz_send, rz_recv, o_sem,
):
    y = lax.axis_index("row")
    z = lax.axis_index("inner")
    o = lax.axis_index("out")
    core = lax.rem(o, 2)
    x = lax.rem(o // 2, NX)
    z = z + Z_LO * (o // (2 * NX))

    def at(dx=0, dy=0, dz=0, dc=0):
        xx = lax.rem(x + dx, NX)
        zz = lax.rem(z + dz, NZ)
        cc = lax.rem(core + dc, 2)
        return (
            lax.rem(y + dy, NY),
            lax.rem(zz, Z_LO),
            ((zz // Z_LO) * NX + xx) * 2 + cc,
        )

    def send(src, dst, ssem, rsem, to):
        copy = pltpu.make_async_remote_copy(
            src_ref=src, dst_ref=dst, send_sem=ssem, recv_sem=rsem,
            device_id=to, device_id_type=MESH,
        )
        copy.start()

    def wait(ref, sem):
        pltpu.make_async_copy(ref, ref, sem).wait()

    pltpu.make_async_copy(tok_in, tok, in_sem.at[0]).start()
    pltpu.make_async_copy(gout_in, gout, in_sem.at[1]).start()
    barrier = pltpu.get_barrier_semaphore()
    peers = (
        [at(dz=d) for d in range(1, NZ)]
        + [at(dx=d) for d in range(1, NX)]
        + [at(dy=d) for d in (range(1, NY) if NEAR1 or NEAR2 else (1, 2, NY - 2, NY - 1))]
        + [at(dc=1)]
    )
    for peer in peers:
        pl.semaphore_signal(barrier, inc=1, device_id=peer, device_id_type=MESH)

    weights = ((wg_in, Wg), (wu_in, Wu), (wd_in, Wd))
    for i, (src, dst) in enumerate(weights):
        pltpu.make_async_copy(src, dst.at[0], w_sem.at[i]).start()

    pltpu.make_async_copy(tok_in, tok, in_sem.at[0]).wait()
    pltpu.make_async_copy(gout_in, gout, in_sem.at[1]).wait()
    here = Z_ORDER.index(0)
    X[here, 0] = jnp.concatenate([tok[...].astype(F32), gout[...].astype(F32)], axis=0).astype(BF16)

    pl.semaphore_wait(barrier, len(peers))

    def to_x(p):
        for dx in (2, 1, 3):
            send(X.at[p, 0], X.at[p, NX - dx], x_send, x_recv.at[p // NG], at(dx=dx))

    for dz in Z_SENDS:
        send(X.at[here, 0], X.at[Z_ORDER.index(NZ - dz), 0], z_send, z_recv.at[NZ - dz - 1], at(dz=dz))
    to_x(here)
    partner = at(dc=1)
    for i, (src, dst) in enumerate(weights):
        send(src, dst.at[1], wx_send.at[i], wx_recv.at[i], partner)

    def pass_on(k):
        for p in range(NG * k, NG * (k + 1)):
            if p != here:
                wait(X.at[p, 0], z_recv.at[Z_ORDER[p] - 1])
                to_x(p)

    low = lax.broadcasted_iota(jnp.int32, (NZ // 2, 8, D), 1) < TB

    def front(j):
        wait(RX.at[0], x_recv.at[j])
        rows = pl.ds(CT * j, CT)
        v = X[NG * j : NG * (j + 1)].astype(F32).reshape(NZ // 2, 2, 8, D)
        even, odd = v[:, 0], v[:, 1]
        t = jnp.where(low, even, pltpu.roll(odd, TB, 1)).reshape(CT, D).astype(BF16)
        g = jnp.where(low, pltpu.roll(even, TB, 1), odd).reshape(CT, D).astype(BF16)
        T[0, rows] = t
        G[0, rows] = g
        send(T.at[0, rows], T.at[1, rows], t_send.at[0], t_recv.at[0], partner)
        send(G.at[0, rows], G.at[1, rows], t_send.at[1], t_recv.at[1], partner)
        for h in range(2):
            if j == 0:
                for i, (src, dst) in enumerate(weights):
                    wait(dst.at[h], (wx_recv if h else w_sem).at[i])
            parts = (dot(t, Wg[h]), dot(t, Wu[h]), dot_nt(g, Wd[h]))
            for half in range(2):
                for c in range(2):
                    q = 4 * half + 2 * h + c
                    for a, part in enumerate(parts):
                        S1[j, q, a] = coded4(
                            part[ROWS * half : ROWS * (half + 1), LANES * c : LANES * (c + 1)]
                        )
        if j in NEAR1:
            for d in (4, 3, 5, 2, 6, 1, 7):
                send(S1.at[j, around(d)], R1.at[j, NY - d - 1], y1_send.at[j], y1_recv.at[j], at(dy=d))
            return
        via = 2 if j % 2 == 0 else -2
        for to, q, dst, sem in (
            (via, 4, K1.at[j, 2], k1_recv),
            (1, 3, K1.at[j, 0], k1_recv),
            (-1, -3, K1.at[j, 1], k1_recv),
            (1, 1, R1.at[j, 0], y1_recv),
            (-1, -1, R1.at[j, 1], y1_recv),
        ):
            send(S1.at[j, around(q)], dst, y1_send.at[j], sem.at[j], at(dy=to % NY))

    def around(d):
        return lax.rem(y + d % NY, NY)

    def relay(j):
        if j in NEAR1:
            return
        wait(K1.at[j], k1_recv.at[j])
        for i, to in enumerate((2, -2)):
            v = decoded4(S1[j, around(to)]) + decoded4(K1[j, i])
            if i == j % 2:
                v += decoded4(K1[j, 2])
            S2[j, i] = coded4(v)
            send(S2.at[j, i], R1.at[j, 2 + i], y1_send.at[j], y1_recv.at[j], at(dy=to % NY))

    def middle(j):
        came = NY - 1 if j in NEAR1 else 4
        wait(R1.at[j, pl.ds(0, came)], y1_recv.at[j])
        gate, up, back = (
            decoded4(S1[j, y, a]) + jnp.sum(decoded4(R1[j, :came, a]), axis=0)
            for a in range(3)
        )
        sig = jax.nn.sigmoid(gate)
        R2[j, y, 0] = (gate * sig * up).astype(BF16)
        R2[j, y, 1] = (back * up * sig * (1.0 + gate * (1.0 - sig))).astype(BF16)
        R2[j, y, 2] = (back * gate * sig).astype(BF16)
        if j in NEAR2:
            for d in (4, 3, 5, 2, 6, 1, 7):
                send(R2.at[j, y], R2.at[j, y], y2_send.at[j], y2_recv.at[j], at(dy=d))
            return
        for to, sem in ((2, k2_recv), (-2, k2_recv), (1, y2_recv), (-1, y2_recv)):
            send(R2.at[j, y], R2.at[j, y], y2_send.at[j], sem.at[j], at(dy=to % NY))

    def spread(j):
        if j in NEAR2:
            return
        wait(R2.at[j, pl.ds(0, 2)], k2_recv.at[j])
        via = 2 if j % 2 == 0 else -2
        for to, q in ((via, -via), (1, -2), (-1, 2)):
            block = R2.at[j, around(q)]
            send(block, block, y2_send.at[j], y2_recv.at[j], at(dy=to % NY))

    def back_end(j):
        wait(R2.at[j, pl.ds(0, NY - 1 if j in NEAR2 else NY - 3)], y2_recv.at[j])
        rows = pl.ds(CT * j, CT)
        full = []
        for a in range(3):
            v = jnp.concatenate(
                [
                    jnp.concatenate([R2[j, 4 * half + c, a].astype(F32) for c in range(4)], axis=1)
                    for half in range(2)
                ],
                axis=0,
            ).astype(BF16)
            own, other = v[:, :F], v[:, F:]
            H[0, a, rows] = own
            HP[a, rows] = other
            full.append((own, other))
        for a in range(3):
            send(HP.at[a, rows], H.at[1, a, rows], h_send.at[a], h_recv.at[a], partner)
        (h0, h1), (g0, g1), (u0, u1) = full
        m = (dot(h0, Wd[0]) + dot(h1, Wd[1])).reshape(NZ // 2, 8, D)
        n = (dot_nt(g0, Wg[0]) + dot_nt(g1, Wg[1]) + dot_nt(u0, Wu[0]) + dot_nt(u1, Wu[1])).reshape(NZ // 2, 8, D)
        even = jnp.where(low, m, pltpu.roll(n, TB, 1))
        odd = jnp.where(low, pltpu.roll(m, TB, 1), n)
        for b in range(NZ):
            v = (odd if b % 2 else even)[b // 2]
            g, dx = b // NX, b % NX
            if dx:
                SX[j, dx - 1, g] = coded2(v)
            else:
                OX[j, g] = v
        for dx in (2, 1, 3):
            send(SX.at[j, dx - 1], RX.at[j, NX - dx - 1], rx_send.at[j], rx_recv.at[j], at(dx=dx))

    def finish(j):
        wait(RX.at[j], rx_recv.at[j])
        own = None
        for g in range(NG):
            dz = Z_ORDER[NG * j + g]
            v = OX[j, g] + jnp.sum(decoded2(RX[j, :, g]), axis=0)
            if dz:
                SZ[dz - 1] = coded2(v)
                send(SZ.at[dz - 1], RZ.at[NZ - dz - 1], rz_send, rz_recv, at(dz=dz))
            else:
                OZ[...] = v

    def turn(i):
        if i == 0:
            wait(T.at[1], t_recv.at[0])
        half = D // 2
        TT[half * i : half * (i + 1)] = T[:, :, half * i : half * (i + 1)].reshape(2 * NC * CT, half).T

    def weight_grad(a):
        b = (a + 1) % 3
        wait(H.at[1, b], h_recv.at[b])
        h = H[:, b].reshape(2 * NC * CT, F)
        if a == 2:
            wait(G.at[1], t_recv.at[1])
            grad = dot_tn(h, G[...].reshape(2 * NC * CT, D))
        else:
            grad = dot(TT[...], h)
        buf, out = ((A1, ggate), (A2, gup), (A3, gdown))[a]
        buf[...] = grad.astype(BF16)
        pltpu.make_async_copy(buf, out, o_sem.at[a]).start()

    stages = dict(
        pass_on=pass_on, front=front, relay=relay, middle=middle, spread=spread, back_end=back_end, finish=finish,
        turn=turn, weight_grad=weight_grad,
    )
    for stage, *chunks in SCHEDULE:
        for chunk in chunks:
            stages[stage](chunk)

    wait(RZ, rz_recv)
    total = OZ[...] + jnp.sum(decoded2(RZ[...]), axis=0)
    tok[...] = total[:TB].astype(BF16)
    gout[...] = total[TB:].astype(BF16)
    pltpu.make_async_copy(tok, mixed, o_sem.at[3]).start()
    pltpu.make_async_copy(gout, gtok, o_sem.at[4]).start()

    wait(RZ, z_send)
    wait(X.at[pl.ds(0, NZ - NG)], x_send)
    wait(RZ, rz_send)
    for i, (src, dst) in enumerate(weights):
        wait(dst.at[0], wx_send.at[i])
    wait(T.at[0], t_send.at[0])
    wait(G.at[0], t_send.at[1])
    for a in range(3):
        wait(HP.at[a], h_send.at[a])
    for j in range(NC):
        wait(SX.at[j], rx_send.at[j])
        wait(R2.at[j, pl.ds(0, 7)], y1_send.at[j])
        wait(R2.at[j, pl.ds(0, 7)], y2_send.at[j])
    for a, (buf, out) in enumerate(((A1, ggate), (A2, gup), (A3, gdown), (tok, mixed), (gout, gtok))):
        pltpu.make_async_copy(buf, out, o_sem.at[a]).wait()


def store(*refs):
    n = (len(refs) - 2) // 3
    src, dst, held, (read, write) = refs[:n], refs[n : 2 * n], refs[2 * n : 3 * n], refs[3 * n :]
    for i in range(n):
        pltpu.make_async_copy(src[i], held[i], read.at[i]).start()
    for i in range(n):
        pltpu.make_async_copy(src[i], held[i], read.at[i]).wait()
        pltpu.make_async_copy(held[i], dst[i], write.at[i]).start()
    for i in range(n):
        pltpu.make_async_copy(held[i], dst[i], write.at[i]).wait()


def on_device(tokens, grad_out, gate_weight, up_weight, down_weight):
    vmem = pl.BlockSpec(memory_space=pltpu.VMEM)
    hbm = pl.BlockSpec(memory_space=pltpu.HBM)
    dma = pltpu.SemaphoreType.DMA
    out_shape = tuple(
        jax.ShapeDtypeStruct(shape, BF16) for shape in ((TB, D), (TB, D), (D, F), (D, F), (F, D))
    )
    outs = pl.pallas_call(
        kernel,
        name="ffn",
        out_shape=out_shape,
        in_specs=[hbm, hbm, hbm, hbm, hbm],
        out_specs=(hbm,) * 5,
        scratch_shapes=[
            pltpu.VMEM((TB, D), BF16),
            pltpu.VMEM((TB, D), BF16),
            pltpu.VMEM((NZ, NX, 8, D), BF16),
            pltpu.VMEM((2, D, F), BF16),
            pltpu.VMEM((2, D, F), BF16),
            pltpu.VMEM((2, F, D), BF16),
            pltpu.VMEM((2, NC * CT, D), BF16),
            pltpu.VMEM((2, NC * CT, D), BF16),
            pltpu.VMEM((D, 2 * NC * CT), BF16),
            pltpu.VMEM((NC, NY, 3, ROWS, LANES), BF16),
            pltpu.VMEM((NC, 3, 3, ROWS, LANES), BF16),
            pltpu.VMEM((NC, 2, 3, ROWS, LANES), BF16),
            pltpu.VMEM((NC, NY - 1, 3, ROWS, LANES), BF16),
            pltpu.VMEM((NC, NY, 3, ROWS, LANES), BF16),
            pltpu.VMEM((2, 3, NC * CT, F), BF16),
            pltpu.VMEM((3, NC * CT, F), BF16),
            pltpu.VMEM((NC, NX - 1, NG, 8, D), BF16),
            pltpu.VMEM((NC, NX - 1, NG, 8, D), BF16),
            pltpu.VMEM((NC, NG, 8, D), F32),
            pltpu.VMEM((8, D), F32),
            pltpu.VMEM((NZ - 1, 8, D), BF16),
            pltpu.VMEM((NZ - 1, 8, D), BF16),
            pltpu.VMEM((D, F), BF16),
            pltpu.VMEM((D, F), BF16),
            pltpu.VMEM((F, D), BF16),
            dma((2,)),
            dma((3,)),
            dma((3,)),
            dma((3,)),
            dma,
            dma((NZ - 1,)),
            dma,
            dma((NC,)),
            dma((2,)),
            dma((2,)),
            dma((NX,)),
            dma((NX,)),
            dma((NX,)),
            dma((NX,)),
            dma((NX,)),
            dma((NX,)),
            dma((3,)),
            dma((3,)),
            dma((NC,)),
            dma((NC,)),
            dma,
            dma,
            dma((5,)),
        ],
        compiler_params=pltpu.CompilerParams(
            collective_id=0, has_side_effects=True, vmem_limit_bytes=62 * 2**20
        ),
        cost_estimate=pl.CostEstimate(
            flops=18 * 384 * D * F, bytes_accessed=2**23, transcendentals=2**17
        ),
    )(tokens, grad_out, gate_weight, up_weight, down_weight)
    return pl.pallas_call(
        store,
        name="store",
        out_shape=out_shape,
        in_specs=[hbm] * 5,
        out_specs=(hbm,) * 5,
        scratch_shapes=[pltpu.VMEM(o.shape, o.dtype) for o in out_shape] + [dma((5,)), dma((5,))],
        compiler_params=pltpu.CompilerParams(vmem_limit_bytes=62 * 2**20),
    )(*outs)


def solution(mesh):
    by_token = P(("inner", "out"), "row")
    by_hidden = P("row", ("inner", "out"))
    return jax.shard_map(
        on_device,
        mesh=mesh,
        in_specs=(by_token, by_token, by_hidden, by_hidden, by_token),
        out_specs=(by_token, by_token, by_hidden, by_hidden, by_token),
        check_vma=False,
    )
```

```python
import functools

import jax
import jax.numpy as jnp
from jax import lax
from jax.experimental import pallas as pl
from jax.experimental.pallas import tpu as pltpu
from jax.sharding import PartitionSpec as P

MESH = pl.DeviceIdType.MESH
BF16, F32 = jnp.bfloat16, jnp.float32

NX, NY, NZ = 4, 8, 12
Z_LO = 6
TB = 4
D = 1024
F = 256
CT = NZ * TB
ROWS, LANES = CT // 2, 128
KNEE4, KNEE2 = 2.0**-12, 2.0**-30
NC, NG = 4, NZ // 4
Z_ORDER = (0, 1, 11, 6, 5, 7, 4, 8, 3, 9, 2, 10)
Z_SENDS = tuple(NZ - dz for dz in Z_ORDER if dz)
SCHEDULE = (
    ("pass_on", 0, 1, 2, 3),
    ("front", 0, 1, 2, 3),
    ("relay", 1, 2, 3, 0),
    ("turn", 0),
    ("middle", 1, 2, 3, 0),
    ("turn", 1),
    ("spread", 1, 2, 3, 0),
    ("back_end", 1, 2, 3, 0),
    ("finish", 1, 2, 3, 0),
    ("weight_grad", 0, 1, 2),
)
NEAR1 = ()
NEAR2 = ()


def dot(a, b):
    return jnp.dot(a, b, preferred_element_type=F32)


def dot_nt(a, b):
    return lax.dot_general(a, b, (((1,), (1,)), ((), ())), preferred_element_type=F32)


def dot_tn(a, b):
    return lax.dot_general(a, b, (((0,), (0,)), ((), ())), preferred_element_type=F32)


def coded4(v):
    r = jnp.maximum(jnp.abs(v) * (1.0 / KNEE4), 1.0)
    return (v * (r * r * r)).astype(BF16)


def decoded4(c):
    c = c.astype(F32)
    root = lax.rsqrt(jnp.maximum(jnp.abs(c) * (1.0 / KNEE4), 1.0))
    return c * (root * jnp.sqrt(root))


def coded2(v):
    return (v * jnp.maximum(jnp.abs(v) * (1.0 / KNEE2), 1.0)).astype(BF16)


def decoded2(c):
    c = c.astype(F32)
    return c * lax.rsqrt(jnp.maximum(jnp.abs(c) * (1.0 / KNEE2), 1.0))


def kernel(
    tok_in, gout_in, wg_in, wu_in, wd_in,
    mixed, gtok, ggate, gup, gdown,
    tok, gout, X, Wg, Wu, Wd, T, G, TT, S1, K1, S2, R1, R2, H, HP, SX, RX, OX, OZ, SZ, RZ, A1, A2, A3,
    in_sem, w_sem, wx_send, wx_recv, z_send, z_recv, x_send, x_recv, t_send, t_recv,
    k1_recv, y1_send, y1_recv, y2_send, k2_recv, y2_recv, h_send, h_recv,
    rx_send, rx_recv, rz_send, rz_recv, o_sem,
):
    y = lax.axis_index("row")
    z = lax.axis_index("inner")
    o = lax.axis_index("out")
    core = lax.rem(o, 2)
    x = lax.rem(o // 2, NX)
    z = z + Z_LO * (o // (2 * NX))

    def at(dx=0, dy=0, dz=0, dc=0):
        xx = lax.rem(x + dx, NX)
        zz = lax.rem(z + dz, NZ)
        cc = lax.rem(core + dc, 2)
        return (
            lax.rem(y + dy, NY),
            lax.rem(zz, Z_LO),
            ((zz // Z_LO) * NX + xx) * 2 + cc,
        )

    def send(src, dst, ssem, rsem, to):
        copy = pltpu.make_async_remote_copy(
            src_ref=src, dst_ref=dst, send_sem=ssem, recv_sem=rsem,
            device_id=to, device_id_type=MESH,
        )
        copy.start()

    def wait(ref, sem):
        pltpu.make_async_copy(ref, ref, sem).wait()

    pltpu.make_async_copy(tok_in, tok, in_sem.at[0]).start()
    pltpu.make_async_copy(gout_in, gout, in_sem.at[1]).start()
    barrier = pltpu.get_barrier_semaphore()
    peers = (
        [at(dz=d) for d in range(1, NZ)]
        + [at(dx=d) for d in range(1, NX)]
        + [at(dy=d) for d in (range(1, NY) if NEAR1 or NEAR2 else (1, 2, NY - 2, NY - 1))]
        + [at(dc=1)]
    )
    for peer in peers:
        pl.semaphore_signal(barrier, inc=1, device_id=peer, device_id_type=MESH)

    weights = ((wg_in, Wg), (wu_in, Wu), (wd_in, Wd))
    for i, (src, dst) in enumerate(weights):
        pltpu.make_async_copy(src, dst.at[0], w_sem.at[i]).start()

    pltpu.make_async_copy(tok_in, tok, in_sem.at[0]).wait()
    pltpu.make_async_copy(gout_in, gout, in_sem.at[1]).wait()
    here = Z_ORDER.index(0)
    X[here, 0] = jnp.concatenate([tok[...].astype(F32), gout[...].astype(F32)], axis=0).astype(BF16)

    pl.semaphore_wait(barrier, len(peers))

    def to_x(p):
        for dx in (2, 1, 3):
            send(X.at[p, 0], X.at[p, NX - dx], x_send, x_recv.at[p // NG], at(dx=dx))

    for dz in Z_SENDS:
        send(X.at[here, 0], X.at[Z_ORDER.index(NZ - dz), 0], z_send, z_recv.at[NZ - dz - 1], at(dz=dz))
    to_x(here)
    partner = at(dc=1)
    for i, (src, dst) in enumerate(weights):
        send(src, dst.at[1], wx_send.at[i], wx_recv.at[i], partner)

    def pass_on(k):
        for p in range(NG * k, NG * (k + 1)):
            if p != here:
                wait(X.at[p, 0], z_recv.at[Z_ORDER[p] - 1])
                to_x(p)

    low = lax.broadcasted_iota(jnp.int32, (NZ // 2, 8, D), 1) < TB

    def front(j):
        wait(RX.at[0], x_recv.at[j])
        rows = pl.ds(CT * j, CT)
        v = X[NG * j : NG * (j + 1)].astype(F32).reshape(NZ // 2, 2, 8, D)
        even, odd = v[:, 0], v[:, 1]
        t = jnp.where(low, even, pltpu.roll(odd, TB, 1)).reshape(CT, D).astype(BF16)
        g = jnp.where(low, pltpu.roll(even, TB, 1), odd).reshape(CT, D).astype(BF16)
        T[0, rows] = t
        G[0, rows] = g
        send(T.at[0, rows], T.at[1, rows], t_send.at[0], t_recv.at[0], partner)
        send(G.at[0, rows], G.at[1, rows], t_send.at[1], t_recv.at[1], partner)
        for h in range(2):
            if j == 0:
                for i, (src, dst) in enumerate(weights):
                    wait(dst.at[h], (wx_recv if h else w_sem).at[i])
            parts = (dot(t, Wg[h]), dot(t, Wu[h]), dot_nt(g, Wd[h]))
            for half in range(2):
                for c in range(2):
                    q = 4 * half + 2 * h + c
                    for a, part in enumerate(parts):
                        S1[j, q, a] = coded4(
                            part[ROWS * half : ROWS * (half + 1), LANES * c : LANES * (c + 1)]
                        )
        if j in NEAR1:
            for d in (4, 3, 5, 2, 6, 1, 7):
                send(S1.at[j, around(d)], R1.at[j, NY - d - 1], y1_send.at[j], y1_recv.at[j], at(dy=d))
            return
        via = 2 if j % 2 == 0 else -2
        for to, q, dst, sem in (
            (via, 4, K1.at[j, 2], k1_recv),
            (1, 3, K1.at[j, 0], k1_recv),
            (-1, -3, K1.at[j, 1], k1_recv),
            (1, 1, R1.at[j, 0], y1_recv),
            (-1, -1, R1.at[j, 1], y1_recv),
        ):
            send(S1.at[j, around(q)], dst, y1_send.at[j], sem.at[j], at(dy=to % NY))

    def around(d):
        return lax.rem(y + d % NY, NY)

    def relay(j):
        if j in NEAR1:
            return
        wait(K1.at[j], k1_recv.at[j])
        for i, to in enumerate((2, -2)):
            v = decoded4(S1[j, around(to)]) + decoded4(K1[j, i])
            if i == j % 2:
                v += decoded4(K1[j, 2])
            S2[j, i] = coded4(v)
            send(S2.at[j, i], R1.at[j, 2 + i], y1_send.at[j], y1_recv.at[j], at(dy=to % NY))

    def middle(j):
        came = NY - 1 if j in NEAR1 else 4
        wait(R1.at[j, pl.ds(0, came)], y1_recv.at[j])
        gate, up, back = (
            decoded4(S1[j, y, a]) + jnp.sum(decoded4(R1[j, :came, a]), axis=0)
            for a in range(3)
        )
        sig = jax.nn.sigmoid(gate)
        R2[j, y, 0] = (gate * sig * up).astype(BF16)
        R2[j, y, 1] = (back * up * sig * (1.0 + gate * (1.0 - sig))).astype(BF16)
        R2[j, y, 2] = (back * gate * sig).astype(BF16)
        if j in NEAR2:
            for d in (4, 3, 5, 2, 6, 1, 7):
                send(R2.at[j, y], R2.at[j, y], y2_send.at[j], y2_recv.at[j], at(dy=d))
            return
        for to, sem in ((2, k2_recv), (-2, k2_recv), (1, y2_recv), (-1, y2_recv)):
            send(R2.at[j, y], R2.at[j, y], y2_send.at[j], sem.at[j], at(dy=to % NY))

    def spread(j):
        if j in NEAR2:
            return
        wait(R2.at[j, pl.ds(0, 2)], k2_recv.at[j])
        via = 2 if j % 2 == 0 else -2
        for to, q in ((via, -via), (1, -2), (-1, 2)):
            block = R2.at[j, around(q)]
            send(block, block, y2_send.at[j], y2_recv.at[j], at(dy=to % NY))

    def back_end(j):
        wait(R2.at[j, pl.ds(0, NY - 1 if j in NEAR2 else NY - 3)], y2_recv.at[j])
        rows = pl.ds(CT * j, CT)
        full = []
        for a in range(3):
            v = jnp.concatenate(
                [
                    jnp.concatenate([R2[j, 4 * half + c, a].astype(F32) for c in range(4)], axis=1)
                    for half in range(2)
                ],
                axis=0,
            ).astype(BF16)
            own, other = v[:, :F], v[:, F:]
            H[0, a, rows] = own
            HP[a, rows] = other
            full.append((own, other))
        for a in range(3):
            send(HP.at[a, rows], H.at[1, a, rows], h_send.at[a], h_recv.at[a], partner)
        (h0, h1), (g0, g1), (u0, u1) = full
        m = (dot(h0, Wd[0]) + dot(h1, Wd[1])).reshape(NZ // 2, 8, D)
        n = (dot_nt(g0, Wg[0]) + dot_nt(g1, Wg[1]) + dot_nt(u0, Wu[0]) + dot_nt(u1, Wu[1])).reshape(NZ // 2, 8, D)
        even = jnp.where(low, m, pltpu.roll(n, TB, 1))
        odd = jnp.where(low, pltpu.roll(m, TB, 1), n)
        for b in range(NZ):
            v = (odd if b % 2 else even)[b // 2]
            g, dx = b // NX, b % NX
            if dx:
                SX[j, dx - 1, g] = coded2(v)
            else:
                OX[j, g] = v
        for dx in (2, 1, 3):
            send(SX.at[j, dx - 1], RX.at[j, NX - dx - 1], rx_send.at[j], rx_recv.at[j], at(dx=dx))

    def finish(j):
        wait(RX.at[j], rx_recv.at[j])
        own = None
        for g in range(NG):
            dz = Z_ORDER[NG * j + g]
            v = OX[j, g] + jnp.sum(decoded2(RX[j, :, g]), axis=0)
            if dz:
                SZ[dz - 1] = coded2(v)
                send(SZ.at[dz - 1], RZ.at[NZ - dz - 1], rz_send, rz_recv, at(dz=dz))
            else:
                OZ[...] = v

    def turn(i):
        if i == 0:
            wait(T.at[1], t_recv.at[0])
        half = D // 2
        TT[half * i : half * (i + 1)] = T[:, :, half * i : half * (i + 1)].reshape(2 * NC * CT, half).T

    def weight_grad(a):
        b = (a + 1) % 3
        wait(H.at[1, b], h_recv.at[b])
        h = H[:, b].reshape(2 * NC * CT, F)
        if a == 2:
            wait(G.at[1], t_recv.at[1])
            grad = dot_tn(h, G[...].reshape(2 * NC * CT, D))
        else:
            grad = dot(TT[...], h)
        buf, out = ((A1, ggate), (A2, gup), (A3, gdown))[a]
        buf[...] = grad.astype(BF16)
        pltpu.make_async_copy(buf, out, o_sem.at[a]).start()

    stages = dict(
        pass_on=pass_on, front=front, relay=relay, middle=middle, spread=spread, back_end=back_end, finish=finish,
        turn=turn, weight_grad=weight_grad,
    )
    for stage, *chunks in SCHEDULE:
        for chunk in chunks:
            stages[stage](chunk)

    wait(RZ, rz_recv)
    total = OZ[...] + jnp.sum(decoded2(RZ[...]), axis=0)
    tok[...] = total[:TB].astype(BF16)
    gout[...] = total[TB:].astype(BF16)
    pltpu.make_async_copy(tok, mixed, o_sem.at[3]).start()
    pltpu.make_async_copy(gout, gtok, o_sem.at[4]).start()

    wait(RZ, z_send)
    wait(X.at[pl.ds(0, NZ - NG)], x_send)
    wait(RZ, rz_send)
    for i, (src, dst) in enumerate(weights):
        wait(dst.at[0], wx_send.at[i])
    wait(T.at[0], t_send.at[0])
    wait(G.at[0], t_send.at[1])
    for a in range(3):
        wait(HP.at[a], h_send.at[a])
    for j in range(NC):
        wait(SX.at[j], rx_send.at[j])
        wait(R2.at[j, pl.ds(0, 7)], y1_send.at[j])
        wait(R2.at[j, pl.ds(0, 7)], y2_send.at[j])
    for a, (buf, out) in enumerate(((A1, ggate), (A2, gup), (A3, gdown), (tok, mixed), (gout, gtok))):
        pltpu.make_async_copy(buf, out, o_sem.at[a]).wait()


PIECES = 4


def store(*refs):
    n = (len(refs) - 2) // 3
    read, write = refs[3 * n :]
    parts = []
    for i in range(n):
        rows = refs[i].shape[0]
        step = rows // PIECES if rows > TB else rows
        for k in range(rows // step):
            part = pl.ds(k * step, step)
            src, dst, held = (refs[i + m * n].at[part] for m in range(3))
            a, b = read.at[i * PIECES + k], write.at[i * PIECES + k]
            parts.append((pltpu.make_async_copy(src, held, a), pltpu.make_async_copy(held, dst, b)))
    for load, _ in parts:
        load.start()
    for load, save in parts:
        load.wait()
        save.start()
    for _, save in parts:
        save.wait()


def on_device(tokens, grad_out, gate_weight, up_weight, down_weight):
    vmem = pl.BlockSpec(memory_space=pltpu.VMEM)
    hbm = pl.BlockSpec(memory_space=pltpu.HBM)
    dma = pltpu.SemaphoreType.DMA
    out_shape = tuple(
        jax.ShapeDtypeStruct(shape, BF16) for shape in ((TB, D), (TB, D), (D, F), (D, F), (F, D))
    )
    outs = pl.pallas_call(
        kernel,
        name="ffn",
        out_shape=out_shape,
        in_specs=[hbm, hbm, hbm, hbm, hbm],
        out_specs=(hbm,) * 5,
        scratch_shapes=[
            pltpu.VMEM((TB, D), BF16),
            pltpu.VMEM((TB, D), BF16),
            pltpu.VMEM((NZ, NX, 8, D), BF16),
            pltpu.VMEM((2, D, F), BF16),
            pltpu.VMEM((2, D, F), BF16),
            pltpu.VMEM((2, F, D), BF16),
            pltpu.VMEM((2, NC * CT, D), BF16),
            pltpu.VMEM((2, NC * CT, D), BF16),
            pltpu.VMEM((D, 2 * NC * CT), BF16),
            pltpu.VMEM((NC, NY, 3, ROWS, LANES), BF16),
            pltpu.VMEM((NC, 3, 3, ROWS, LANES), BF16),
            pltpu.VMEM((NC, 2, 3, ROWS, LANES), BF16),
            pltpu.VMEM((NC, NY - 1, 3, ROWS, LANES), BF16),
            pltpu.VMEM((NC, NY, 3, ROWS, LANES), BF16),
            pltpu.VMEM((2, 3, NC * CT, F), BF16),
            pltpu.VMEM((3, NC * CT, F), BF16),
            pltpu.VMEM((NC, NX - 1, NG, 8, D), BF16),
            pltpu.VMEM((NC, NX - 1, NG, 8, D), BF16),
            pltpu.VMEM((NC, NG, 8, D), F32),
            pltpu.VMEM((8, D), F32),
            pltpu.VMEM((NZ - 1, 8, D), BF16),
            pltpu.VMEM((NZ - 1, 8, D), BF16),
            pltpu.VMEM((D, F), BF16),
            pltpu.VMEM((D, F), BF16),
            pltpu.VMEM((F, D), BF16),
            dma((2,)),
            dma((3,)),
            dma((3,)),
            dma((3,)),
            dma,
            dma((NZ - 1,)),
            dma,
            dma((NC,)),
            dma((2,)),
            dma((2,)),
            dma((NX,)),
            dma((NX,)),
            dma((NX,)),
            dma((NX,)),
            dma((NX,)),
            dma((NX,)),
            dma((3,)),
            dma((3,)),
            dma((NC,)),
            dma((NC,)),
            dma,
            dma,
            dma((5,)),
        ],
        compiler_params=pltpu.CompilerParams(
            collective_id=0, has_side_effects=True, vmem_limit_bytes=62 * 2**20
        ),
        cost_estimate=pl.CostEstimate(
            flops=18 * 384 * D * F, bytes_accessed=2**23, transcendentals=2**17
        ),
    )(tokens, grad_out, gate_weight, up_weight, down_weight)
    return pl.pallas_call(
        store,
        name="store",
        out_shape=out_shape,
        in_specs=[hbm] * 5,
        out_specs=(hbm,) * 5,
        scratch_shapes=[pltpu.VMEM(o.shape, o.dtype) for o in out_shape] + [dma((5 * PIECES,)), dma((5 * PIECES,))],
        compiler_params=pltpu.CompilerParams(vmem_limit_bytes=62 * 2**20),
    )(*outs)


def solution(mesh):
    by_token = P(("inner", "out"), "row")
    by_hidden = P("row", ("inner", "out"))
    return jax.shard_map(
        on_device,
        mesh=mesh,
        in_specs=(by_token, by_token, by_hidden, by_hidden, by_token),
        out_specs=(by_token, by_token, by_hidden, by_hidden, by_token),
        check_vma=False,
    )
```

```python
import functools

import jax
import jax.numpy as jnp
from jax import lax
from jax.experimental import pallas as pl
from jax.experimental.pallas import tpu as pltpu
from jax.sharding import PartitionSpec as P

MESH = pl.DeviceIdType.MESH
BF16, F32 = jnp.bfloat16, jnp.float32

NX, NY, NZ = 4, 8, 12
Z_LO = 6
TB = 4
D = 1024
F = 256
CT = NZ * TB
ROWS, LANES = CT // 2, 128
KNEE4, KNEE2 = 2.0**-12, 2.0**-30
NC, NG = 4, NZ // 4
Z_ORDER = (0, 1, 11, 6, 5, 7, 4, 8, 3, 9, 2, 10)
Z_SENDS = tuple(NZ - dz for dz in Z_ORDER if dz)
SCHEDULE = (
    ("pass_on", 0, 1, 2, 3),
    ("front", 0, 1, 2, 3),
    ("turn", 0),
    ("relay", 0),
    ("middle", 1, 2, 3, 0),
    ("turn", 1),
    ("spread", 1, 2, 3, 0),
    ("back_end", 1, 2, 3, 0),
    ("finish", 1, 2, 3, 0),
    ("weight_grad", 0, 1, 2),
)
NEAR1 = (1, 2, 3)
NEAR2 = ()


def dot(a, b):
    return jnp.dot(a, b, preferred_element_type=F32)


def dot_nt(a, b):
    return lax.dot_general(a, b, (((1,), (1,)), ((), ())), preferred_element_type=F32)


def dot_tn(a, b):
    return lax.dot_general(a, b, (((0,), (0,)), ((), ())), preferred_element_type=F32)


def coded4(v):
    r = jnp.maximum(jnp.abs(v) * (1.0 / KNEE4), 1.0)
    return (v * (r * r * r)).astype(BF16)


def decoded4(c):
    c = c.astype(F32)
    root = lax.rsqrt(jnp.maximum(jnp.abs(c) * (1.0 / KNEE4), 1.0))
    return c * (root * jnp.sqrt(root))


def coded2(v):
    return (v * jnp.maximum(jnp.abs(v) * (1.0 / KNEE2), 1.0)).astype(BF16)


def decoded2(c):
    c = c.astype(F32)
    return c * lax.rsqrt(jnp.maximum(jnp.abs(c) * (1.0 / KNEE2), 1.0))


def kernel(
    tok_in, gout_in, wg_in, wu_in, wd_in,
    mixed, gtok, ggate, gup, gdown,
    tok, gout, X, Wg, Wu, Wd, T, G, TT, S1, K1, S2, R1, R2, H, HP, SX, RX, OX, OZ, SZ, RZ, A1, A2, A3,
    in_sem, w_sem, wx_send, wx_recv, z_send, z_recv, x_send, x_recv, t_send, t_recv,
    k1_recv, y1_send, y1_recv, y2_send, k2_recv, y2_recv, h_send, h_recv,
    rx_send, rx_recv, rz_send, rz_recv, o_sem,
):
    y = lax.axis_index("row")
    z = lax.axis_index("inner")
    o = lax.axis_index("out")
    core = lax.rem(o, 2)
    x = lax.rem(o // 2, NX)
    z = z + Z_LO * (o // (2 * NX))

    def at(dx=0, dy=0, dz=0, dc=0):
        xx = lax.rem(x + dx, NX)
        zz = lax.rem(z + dz, NZ)
        cc = lax.rem(core + dc, 2)
        return (
            lax.rem(y + dy, NY),
            lax.rem(zz, Z_LO),
            ((zz // Z_LO) * NX + xx) * 2 + cc,
        )

    def send(src, dst, ssem, rsem, to):
        copy = pltpu.make_async_remote_copy(
            src_ref=src, dst_ref=dst, send_sem=ssem, recv_sem=rsem,
            device_id=to, device_id_type=MESH,
        )
        copy.start()

    def wait(ref, sem):
        pltpu.make_async_copy(ref, ref, sem).wait()

    pltpu.make_async_copy(tok_in, tok, in_sem.at[0]).start()
    pltpu.make_async_copy(gout_in, gout, in_sem.at[1]).start()
    barrier = pltpu.get_barrier_semaphore()
    peers = (
        [at(dz=d) for d in range(1, NZ)]
        + [at(dx=d) for d in range(1, NX)]
        + [at(dy=d) for d in (range(1, NY) if NEAR1 or NEAR2 else (1, 2, NY - 2, NY - 1))]
        + [at(dc=1)]
    )
    for peer in peers:
        pl.semaphore_signal(barrier, inc=1, device_id=peer, device_id_type=MESH)

    weights = ((wg_in, Wg), (wu_in, Wu), (wd_in, Wd))
    for i, (src, dst) in enumerate(weights):
        pltpu.make_async_copy(src, dst.at[0], w_sem.at[i]).start()

    pltpu.make_async_copy(tok_in, tok, in_sem.at[0]).wait()
    pltpu.make_async_copy(gout_in, gout, in_sem.at[1]).wait()
    here = Z_ORDER.index(0)
    X[here, 0] = jnp.concatenate([tok[...].astype(F32), gout[...].astype(F32)], axis=0).astype(BF16)

    pl.semaphore_wait(barrier, len(peers))

    def to_x(p):
        for dx in (2, 1, 3):
            send(X.at[p, 0], X.at[p, NX - dx], x_send, x_recv.at[p // NG], at(dx=dx))

    for dz in Z_SENDS:
        send(X.at[here, 0], X.at[Z_ORDER.index(NZ - dz), 0], z_send, z_recv.at[NZ - dz - 1], at(dz=dz))
    to_x(here)
    partner = at(dc=1)
    for i, (src, dst) in enumerate(weights):
        send(src, dst.at[1], wx_send.at[i], wx_recv.at[i], partner)

    def pass_on(k):
        for p in range(NG * k, NG * (k + 1)):
            if p != here:
                wait(X.at[p, 0], z_recv.at[Z_ORDER[p] - 1])
                to_x(p)

    low = lax.broadcasted_iota(jnp.int32, (NZ // 2, 8, D), 1) < TB

    def front(j):
        wait(RX.at[0], x_recv.at[j])
        rows = pl.ds(CT * j, CT)
        v = X[NG * j : NG * (j + 1)].astype(F32).reshape(NZ // 2, 2, 8, D)
        even, odd = v[:, 0], v[:, 1]
        t = jnp.where(low, even, pltpu.roll(odd, TB, 1)).reshape(CT, D).astype(BF16)
        g = jnp.where(low, pltpu.roll(even, TB, 1), odd).reshape(CT, D).astype(BF16)
        T[0, rows] = t
        G[0, rows] = g
        send(T.at[0, rows], T.at[1, rows], t_send.at[0], t_recv.at[0], partner)
        send(G.at[0, rows], G.at[1, rows], t_send.at[1], t_recv.at[1], partner)
        for h in range(2):
            if j == 0:
                for i, (src, dst) in enumerate(weights):
                    wait(dst.at[h], (wx_recv if h else w_sem).at[i])
            parts = (dot(t, Wg[h]), dot(t, Wu[h]), dot_nt(g, Wd[h]))
            for half in range(2):
                for c in range(2):
                    q = 4 * half + 2 * h + c
                    for a, part in enumerate(parts):
                        S1[j, q, a] = coded4(
                            part[ROWS * half : ROWS * (half + 1), LANES * c : LANES * (c + 1)]
                        )
        if j in NEAR1:
            for d in (4, 3, 5, 2, 6, 1, 7):
                send(S1.at[j, around(d)], R1.at[j, NY - d - 1], y1_send.at[j], y1_recv.at[j], at(dy=d))
            return
        via = 2 if j % 2 == 0 else -2
        for to, q, dst, sem in (
            (via, 4, K1.at[j, 2], k1_recv),
            (1, 3, K1.at[j, 0], k1_recv),
            (-1, -3, K1.at[j, 1], k1_recv),
            (1, 1, R1.at[j, 0], y1_recv),
            (-1, -1, R1.at[j, 1], y1_recv),
        ):
            send(S1.at[j, around(q)], dst, y1_send.at[j], sem.at[j], at(dy=to % NY))

    def around(d):
        return lax.rem(y + d % NY, NY)

    def relay(j):
        if j in NEAR1:
            return
        wait(K1.at[j], k1_recv.at[j])
        for i, to in enumerate((2, -2)):
            v = decoded4(S1[j, around(to)]) + decoded4(K1[j, i])
            if i == j % 2:
                v += decoded4(K1[j, 2])
            S2[j, i] = coded4(v)
            send(S2.at[j, i], R1.at[j, 2 + i], y1_send.at[j], y1_recv.at[j], at(dy=to % NY))

    def middle(j):
        came = NY - 1 if j in NEAR1 else 4
        wait(R1.at[j, pl.ds(0, came)], y1_recv.at[j])
        gate, up, back = (
            decoded4(S1[j, y, a]) + jnp.sum(decoded4(R1[j, :came, a]), axis=0)
            for a in range(3)
        )
        sig = jax.nn.sigmoid(gate)
        R2[j, y, 0] = (gate * sig * up).astype(BF16)
        R2[j, y, 1] = (back * up * sig * (1.0 + gate * (1.0 - sig))).astype(BF16)
        R2[j, y, 2] = (back * gate * sig).astype(BF16)
        if j in NEAR2:
            for d in (4, 3, 5, 2, 6, 1, 7):
                send(R2.at[j, y], R2.at[j, y], y2_send.at[j], y2_recv.at[j], at(dy=d))
            return
        for to, sem in ((2, k2_recv), (-2, k2_recv), (1, y2_recv), (-1, y2_recv)):
            send(R2.at[j, y], R2.at[j, y], y2_send.at[j], sem.at[j], at(dy=to % NY))

    def spread(j):
        if j in NEAR2:
            return
        wait(R2.at[j, pl.ds(0, 2)], k2_recv.at[j])
        via = 2 if j % 2 == 0 else -2
        for to, q in ((via, -via), (1, -2), (-1, 2)):
            block = R2.at[j, around(q)]
            send(block, block, y2_send.at[j], y2_recv.at[j], at(dy=to % NY))

    def back_end(j):
        wait(R2.at[j, pl.ds(0, NY - 1 if j in NEAR2 else NY - 3)], y2_recv.at[j])
        rows = pl.ds(CT * j, CT)
        full = []
        for a in range(3):
            v = jnp.concatenate(
                [
                    jnp.concatenate([R2[j, 4 * half + c, a].astype(F32) for c in range(4)], axis=1)
                    for half in range(2)
                ],
                axis=0,
            ).astype(BF16)
            own, other = v[:, :F], v[:, F:]
            H[0, a, rows] = own
            HP[a, rows] = other
            full.append((own, other))
        for a in range(3):
            send(HP.at[a, rows], H.at[1, a, rows], h_send.at[a], h_recv.at[a], partner)
        (h0, h1), (g0, g1), (u0, u1) = full
        m = (dot(h0, Wd[0]) + dot(h1, Wd[1])).reshape(NZ // 2, 8, D)
        n = (dot_nt(g0, Wg[0]) + dot_nt(g1, Wg[1]) + dot_nt(u0, Wu[0]) + dot_nt(u1, Wu[1])).reshape(NZ // 2, 8, D)
        even = jnp.where(low, m, pltpu.roll(n, TB, 1))
        odd = jnp.where(low, pltpu.roll(m, TB, 1), n)
        for b in range(NZ):
            v = (odd if b % 2 else even)[b // 2]
            g, dx = b // NX, b % NX
            if dx:
                SX[j, dx - 1, g] = coded2(v)
            else:
                OX[j, g] = v
        for dx in (2, 1, 3):
            send(SX.at[j, dx - 1], RX.at[j, NX - dx - 1], rx_send.at[j], rx_recv.at[j], at(dx=dx))

    def finish(j):
        wait(RX.at[j], rx_recv.at[j])
        own = None
        for g in range(NG):
            dz = Z_ORDER[NG * j + g]
            v = OX[j, g] + jnp.sum(decoded2(RX[j, :, g]), axis=0)
            if dz:
                SZ[dz - 1] = coded2(v)
                send(SZ.at[dz - 1], RZ.at[NZ - dz - 1], rz_send, rz_recv, at(dz=dz))
            else:
                OZ[...] = v

    def turn(i):
        if i == 0:
            wait(T.at[1], t_recv.at[0])
        half = D // 2
        TT[half * i : half * (i + 1)] = T[:, :, half * i : half * (i + 1)].reshape(2 * NC * CT, half).T

    def weight_grad(a):
        b = (a + 1) % 3
        wait(H.at[1, b], h_recv.at[b])
        h = H[:, b].reshape(2 * NC * CT, F)
        if a == 2:
            wait(G.at[1], t_recv.at[1])
            grad = dot_tn(h, G[...].reshape(2 * NC * CT, D))
        else:
            grad = dot(TT[...], h)
        buf, out = ((A1, ggate), (A2, gup), (A3, gdown))[a]
        buf[...] = grad.astype(BF16)
        pltpu.make_async_copy(buf, out, o_sem.at[a]).start()

    stages = dict(
        pass_on=pass_on, front=front, relay=relay, middle=middle, spread=spread, back_end=back_end, finish=finish,
        turn=turn, weight_grad=weight_grad,
    )
    for stage, *chunks in SCHEDULE:
        for chunk in chunks:
            stages[stage](chunk)

    wait(RZ, rz_recv)
    total = OZ[...] + jnp.sum(decoded2(RZ[...]), axis=0)
    tok[...] = total[:TB].astype(BF16)
    gout[...] = total[TB:].astype(BF16)
    pltpu.make_async_copy(tok, mixed, o_sem.at[3]).start()
    pltpu.make_async_copy(gout, gtok, o_sem.at[4]).start()

    wait(RZ, z_send)
    wait(X.at[pl.ds(0, NZ - NG)], x_send)
    wait(RZ, rz_send)
    for i, (src, dst) in enumerate(weights):
        wait(dst.at[0], wx_send.at[i])
    wait(T.at[0], t_send.at[0])
    wait(G.at[0], t_send.at[1])
    for a in range(3):
        wait(HP.at[a], h_send.at[a])
    for j in range(NC):
        wait(SX.at[j], rx_send.at[j])
        wait(R2.at[j, pl.ds(0, 7)], y1_send.at[j])
        wait(R2.at[j, pl.ds(0, 7)], y2_send.at[j])
    for a, (buf, out) in enumerate(((A1, ggate), (A2, gup), (A3, gdown), (tok, mixed), (gout, gtok))):
        pltpu.make_async_copy(buf, out, o_sem.at[a]).wait()


def store(*refs):
    n = (len(refs) - 2) // 3
    src, dst, held, (read, write) = refs[:n], refs[n : 2 * n], refs[2 * n : 3 * n], refs[3 * n :]
    for i in range(n):
        pltpu.make_async_copy(src[i], held[i], read.at[i]).start()
    for i in range(n):
        pltpu.make_async_copy(src[i], held[i], read.at[i]).wait()
        pltpu.make_async_copy(held[i], dst[i], write.at[i]).start()
    for i in range(n):
        pltpu.make_async_copy(held[i], dst[i], write.at[i]).wait()


def on_device(tokens, grad_out, gate_weight, up_weight, down_weight):
    vmem = pl.BlockSpec(memory_space=pltpu.VMEM)
    hbm = pl.BlockSpec(memory_space=pltpu.HBM)
    dma = pltpu.SemaphoreType.DMA
    out_shape = tuple(
        jax.ShapeDtypeStruct(shape, BF16) for shape in ((TB, D), (TB, D), (D, F), (D, F), (F, D))
    )
    outs = pl.pallas_call(
        kernel,
        name="ffn",
        out_shape=out_shape,
        in_specs=[hbm, hbm, hbm, hbm, hbm],
        out_specs=(hbm,) * 5,
        scratch_shapes=[
            pltpu.VMEM((TB, D), BF16),
            pltpu.VMEM((TB, D), BF16),
            pltpu.VMEM((NZ, NX, 8, D), BF16),
            pltpu.VMEM((2, D, F), BF16),
            pltpu.VMEM((2, D, F), BF16),
            pltpu.VMEM((2, F, D), BF16),
            pltpu.VMEM((2, NC * CT, D), BF16),
            pltpu.VMEM((2, NC * CT, D), BF16),
            pltpu.VMEM((D, 2 * NC * CT), BF16),
            pltpu.VMEM((NC, NY, 3, ROWS, LANES), BF16),
            pltpu.VMEM((NC, 3, 3, ROWS, LANES), BF16),
            pltpu.VMEM((NC, 2, 3, ROWS, LANES), BF16),
            pltpu.VMEM((NC, NY - 1, 3, ROWS, LANES), BF16),
            pltpu.VMEM((NC, NY, 3, ROWS, LANES), BF16),
            pltpu.VMEM((2, 3, NC * CT, F), BF16),
            pltpu.VMEM((3, NC * CT, F), BF16),
            pltpu.VMEM((NC, NX - 1, NG, 8, D), BF16),
            pltpu.VMEM((NC, NX - 1, NG, 8, D), BF16),
            pltpu.VMEM((NC, NG, 8, D), F32),
            pltpu.VMEM((8, D), F32),
            pltpu.VMEM((NZ - 1, 8, D), BF16),
            pltpu.VMEM((NZ - 1, 8, D), BF16),
            pltpu.VMEM((D, F), BF16),
            pltpu.VMEM((D, F), BF16),
            pltpu.VMEM((F, D), BF16),
            dma((2,)),
            dma((3,)),
            dma((3,)),
            dma((3,)),
            dma,
            dma((NZ - 1,)),
            dma,
            dma((NC,)),
            dma((2,)),
            dma((2,)),
            dma((NX,)),
            dma((NX,)),
            dma((NX,)),
            dma((NX,)),
            dma((NX,)),
            dma((NX,)),
            dma((3,)),
            dma((3,)),
            dma((NC,)),
            dma((NC,)),
            dma,
            dma,
            dma((5,)),
        ],
        compiler_params=pltpu.CompilerParams(
            collective_id=0, has_side_effects=True, vmem_limit_bytes=62 * 2**20
        ),
        cost_estimate=pl.CostEstimate(
            flops=18 * 384 * D * F, bytes_accessed=2**23, transcendentals=2**17
        ),
    )(tokens, grad_out, gate_weight, up_weight, down_weight)
    return pl.pallas_call(
        store,
        name="store",
        out_shape=out_shape,
        in_specs=[hbm] * 5,
        out_specs=(hbm,) * 5,
        scratch_shapes=[pltpu.VMEM(o.shape, o.dtype) for o in out_shape] + [dma((5,)), dma((5,))],
        compiler_params=pltpu.CompilerParams(vmem_limit_bytes=62 * 2**20),
    )(*outs)


def solution(mesh):
    by_token = P(("inner", "out"), "row")
    by_hidden = P("row", ("inner", "out"))
    return jax.shard_map(
        on_device,
        mesh=mesh,
        in_specs=(by_token, by_token, by_hidden, by_hidden, by_token),
        out_specs=(by_token, by_token, by_hidden, by_hidden, by_token),
        check_vma=False,
    )
```
